32 devices in a mesh: energy: 16 (over z, y, x), slab: 2 (over core).
Axes of the slice: x: 2, y: 2, z: 4, core: 2. Of those that a mesh axis runs over, the one named last changes fastest.
Arguments:
- green_local: bfloat16 [16, 768, 768], P('energy', 'slab'), may hold values from -6 to 6
- coupling: bfloat16 [768, 384], P('slab'), may hold values from -0.3125 to 0.3125
- phonon_coupling: bfloat16 [3, 384, 384], replicated, may hold values from -0.3125 to 0.3125
- offsets: int32 [3], replicated, may hold values from 1 to 4, as said below
- bose_factors: float32 [3], replicated, may hold values from 0.2 to 3
Outputs:
- phonon_sigma: bfloat16 [16, 768, 768], P('energy', 'slab')
- cumulative: float32 [16, 768], P('energy', 'slab')
The draws below stay inside these ranges and needn't reach their ends.
Inputs may be any that keep to these rules, and one draw needn't show every extreme that they name: The offsets are distinct, and one of them equals 4.
All inputs are finite; a program needn't handle non-finite values.
Results may differ from the reference program's by a relative error of at most 0.018.
Values may be sent and summed in bfloat16 or wider, within the bound.
No kernel may reach another device: no remote copies, remote signals or barrier semaphores. Data moves between devices by JAX's collectives and lax.ppermute only.
A program may use at most 64 MiB of HBM per device.

```python
import math
import jax
import jax.numpy as jnp
from jax import lax

M = 384
MODES = 3
OMAX = 4
ENERGIES = 16
SLABS = 2


def draw_offsets(key, part):
    key_one, key_two = jax.random.split(jax.random.fold_in(key, 7))
    smaller = jax.random.permutation(key_one, OMAX - 1) + 1
    chosen = jnp.concatenate([smaller[:MODES - 1], jnp.array([OMAX])])
    return jax.random.permutation(key_two, chosen).astype(jnp.int32)


def level_of(own_key, shape, cuts, smallest, largest):
    def one(position, blocks):
        draws = jax.random.uniform(jax.random.fold_in(jax.random.fold_in(own_key, 6), position), (blocks,), jnp.float32, smallest / len(cuts), largest / len(cuts))
        return jnp.repeat(jnp.exp(draws), shape[position] // blocks).reshape((-1,) + (1,) * (len(shape) - position - 1))

    loudness = one(*cuts[0])
    for cut in cuts[1:]:
        loudness = loudness * one(*cut)
    return loudness


def centred(own_key, shape, spread, bound, pieces=(), kind=jnp.bfloat16):
    result = spread * jax.random.normal(own_key, shape, jnp.float32)
    if pieces:
        result = result * level_of(own_key, shape, pieces, -0.22, 0.18)
    return jnp.clip(result, -bound, bound).astype(kind)


def setup_inputs(seed: int = 0) -> dict:
    seeds = jax.random.split(jax.random.key(seed), 6)
    green_local = centred(seeds[0], (ENERGIES, SLABS * M, 2 * M), 1.0, 6.0, ((0, 16), (1, 2)))
    coupling = centred(seeds[1], (SLABS * M, M), M ** -0.5, 0.3125, ((0, 2),))
    phonon_coupling = centred(seeds[2], (MODES, M, M), M ** -0.5, 0.3125)
    offsets = draw_offsets(jax.random.fold_in(seeds[5], 71), 0)
    bose_factors = jnp.clip(jnp.exp(jax.random.uniform(seeds[4], (MODES,), jnp.float32, math.log(0.2), math.log(3.0))), 0.2, 3.0)
    return dict(green_local=green_local, coupling=coupling, phonon_coupling=phonon_coupling, offsets=offsets, bose_factors=bose_factors)


def left_real(matrices, blocks):
    return jnp.einsum('eab,ebc->eac', matrices.astype(jnp.float32), blocks.astype(jnp.float32))


def right_real(blocks, matrices):
    batch_size, row_count, double = blocks.shape
    halves = blocks.reshape(batch_size, row_count, 2, double // 2).astype(jnp.float32)
    product = jnp.einsum('eatm,emb->eatb', halves, matrices.astype(jnp.float32))
    return product.reshape(batch_size, row_count, double)


def complex_matrix(blocks):
    half_width = blocks.shape[-1] // 2
    real_part = blocks[..., :half_width]
    imag_part = blocks[..., half_width:]
    top_rows = jnp.concatenate([real_part, imag_part], axis=-1)
    bottom_rows = jnp.concatenate([-imag_part, real_part], axis=-1)
    return jnp.concatenate([top_rows, bottom_rows], axis=-2)


def complex_product(first, second):
    return jnp.einsum('eam,emn->ean', first.astype(jnp.float32), complex_matrix(second).astype(jnp.float32))


def reference(green_local, coupling, phonon_coupling, offsets, bose_factors):
    energies = green_local.shape[0]
    blocks = green_local.reshape(energies, SLABS, M, 2 * M)
    links = coupling.reshape(SLABS, M, M)
    links_transposed = jnp.swapaxes(links, 1, 2)
    zero_link = jnp.zeros((1, M, M), jnp.bfloat16)
    lower_links = jnp.concatenate([zero_link, links[:-1]], axis=0)
    lower_transposed = jnp.swapaxes(lower_links, 1, 2)

    def dress(energy_blocks):
        zero_block = jnp.zeros((1, M, 2 * M), jnp.bfloat16)
        upper_blocks = jnp.concatenate([energy_blocks[1:], zero_block], axis=0)
        lower_blocks = jnp.concatenate([zero_block, energy_blocks[:-1]], axis=0)
        up_left = left_real(links, upper_blocks).astype(jnp.bfloat16)
        upper_term = right_real(up_left, links_transposed).astype(jnp.bfloat16)
        down_left = left_real(lower_transposed, lower_blocks).astype(jnp.bfloat16)
        lower_term = right_real(down_left, lower_links).astype(jnp.bfloat16)
        couple = (upper_term.astype(jnp.float32) + lower_term.astype(jnp.float32)).astype(jnp.bfloat16)
        dressed = complex_product(energy_blocks, couple).astype(jnp.bfloat16)
        corrected = energy_blocks.astype(jnp.float32) + complex_product(dressed, energy_blocks) / M
        return corrected.astype(jnp.bfloat16)

    greens = lax.map(dress, blocks)

    positions = jnp.arange(energies, dtype=jnp.int32).astype(jnp.float32)
    holes = jax.nn.sigmoid((positions + 0.5 - energies / 2) * 4.0 / energies)
    imag_diag = jnp.diagonal(greens[..., M:], axis1=2, axis2=3).astype(jnp.float32)
    dos_terms = -holes[:, None, None] * imag_diag
    cumulative = jnp.cumsum(dos_terms, axis=0).reshape(energies, SLABS * M)

    phonon_transposed = jnp.swapaxes(phonon_coupling, 1, 2)

    def self_energy(energy):
        accumulated = jnp.zeros((SLABS, M, 2 * M), jnp.float32)
        for mode_index in range(MODES):
            shift_size = offsets[mode_index]
            below_index = energy - shift_size
            above_index = energy + shift_size
            lower_block = greens[jnp.clip(below_index, 0, energies - 1)].astype(jnp.float32) * (below_index >= 0).astype(jnp.float32)
            upper_block = greens[jnp.clip(above_index, 0, energies - 1)].astype(jnp.float32) * (above_index < energies).astype(jnp.float32)
            factor = bose_factors[mode_index]
            mixture = ((factor + 1.0) * lower_block + factor * upper_block).astype(jnp.bfloat16)
            matrices = jnp.broadcast_to(phonon_coupling[mode_index][None], (SLABS, M, M))
            matrices_transposed = jnp.broadcast_to(phonon_transposed[mode_index][None], (SLABS, M, M))
            phonon_left = left_real(matrices, mixture).astype(jnp.bfloat16)
            accumulated = accumulated + right_real(phonon_left, matrices_transposed)
        return accumulated.astype(jnp.bfloat16)

    phonon_sigma = lax.map(self_energy, jnp.arange(energies, dtype=jnp.int32))
    phonon_sigma = phonon_sigma.reshape(energies, SLABS * M, 2 * M)
    return phonon_sigma, cumulative
```

```python
import functools

import jax
import jax.numpy as jnp
from jax import lax
from jax.experimental import pallas as pl
from jax.experimental.pallas import tpu as pltpu
from jax.sharding import PartitionSpec as P

OMAX = 4
GROUP = OMAX
VMEM_LIMIT = 24 * 1024 * 1024

WHOLE = pl.BlockSpec(memory_space=pltpu.VMEM)
SCALARS = pl.BlockSpec(memory_space=pltpu.SMEM)


def nn(a, b):
    return lax.dot_general(a, b, (((1,), (0,)), ((), ())), preferred_element_type=jnp.float32)


def nt(a, b):
    return lax.dot_general(a, b, (((1,), (1,)), ((), ())), preferred_element_type=jnp.float32)


def tn(a, b):
    return lax.dot_general(a, b, (((0,), (0,)), ((), ())), preferred_element_type=jnp.float32)


def bf(value):
    return value.astype(jnp.bfloat16)


def f32(value):
    return value.astype(jnp.float32)


def call(kernel, outs, ins, scratch, units, m):
    spaces = [SCALARS if i.ndim == 1 else WHOLE for i in ins]
    moved = sum(a.size * a.dtype.itemsize for a in (*ins, *outs))
    return pl.pallas_call(
        kernel,
        out_shape=outs,
        in_specs=spaces,
        out_specs=[WHOLE] * len(outs),
        scratch_shapes=scratch,
        compiler_params=pltpu.CompilerParams(vmem_limit_bytes=VMEM_LIMIT),
        cost_estimate=pl.CostEstimate(
            flops=2 * units * m * m * m, bytes_accessed=moved, transcendentals=0
        ),
    )(*ins)


def upper_term(link, block):
    m = link.shape[0]
    left = bf(nn(link, block))
    return bf(nt(left[:, :m], link)), bf(nt(left[:, m:], link))


def lower_term(link, block):
    m = link.shape[0]
    left = bf(tn(link, block))
    return bf(nn(left[:, :m], link)), bf(nn(left[:, m:], link))


def finish_greens(g, real, imag, greens_real, greens_imag):
    m = g.shape[0]
    g_real, g_imag = g[:, :m], g[:, m:]
    dressed = bf(
        nn(g_real, jnp.concatenate([real, imag], axis=1))
        + nn(g_imag, jnp.concatenate([-imag, real], axis=1))
    )
    swapped = jnp.concatenate([-g_imag, g_real], axis=1)
    greens = bf(f32(g) + (nn(dressed[:, :m], g) + nn(dressed[:, m:], swapped)) / m)
    greens_real[...] = greens[:, :m]
    greens_imag[...] = greens[:, m:]


def greens_of_pair(g_ref, other_ref, own_ref, below_ref, real_ref, imag_ref, couple):
    m = own_ref.shape[0]
    slab = lax.axis_index("slab")

    @pl.when(slab == 0)
    def _():
        real, imag = upper_term(own_ref[...], other_ref[...])
        couple[:, :m] = real
        couple[:, m:] = imag

    @pl.when(slab != 0)
    def _():
        real, imag = lower_term(below_ref[...], other_ref[...])
        couple[:, :m] = real
        couple[:, m:] = imag

    finish_greens(g_ref[...], couple[:, :m], couple[:, m:], real_ref, imag_ref)


def greens_of_chain(g_ref, above_ref, lower_ref, own_ref, below_ref, real_ref, imag_ref):
    up_real, up_imag = upper_term(own_ref[...], above_ref[...])
    low_real, low_imag = lower_term(below_ref[...], lower_ref[...])
    real = bf(f32(up_real) + f32(low_real))
    imag = bf(f32(up_imag) + f32(low_imag))
    finish_greens(g_ref[...], real, imag, real_ref, imag_ref)


def greens_halves(g, coupling):
    m = g.shape[0]
    slabs = lax.axis_size("slab")
    half = jax.ShapeDtypeStruct((m, m), jnp.bfloat16)
    up = [(s, s + 1) for s in range(slabs - 1)]
    down = [(s + 1, s) for s in range(slabs - 1)]
    if slabs == 2:
        other = lax.ppermute(g, "slab", up + down)
        below = lax.ppermute(coupling, "slab", up)
        scratch = [pltpu.VMEM(g.shape, jnp.bfloat16)]
        return call(greens_of_pair, [half] * 2, [g, other, coupling, below], scratch, 12, m)
    above = lax.ppermute(g, "slab", down)
    lower = lax.ppermute(g, "slab", up)
    below = lax.ppermute(coupling, "slab", up)
    return call(greens_of_chain, [half] * 2, [g, above, lower, coupling, below], [], 16, m)


def place():
    energy = lax.axis_index("energy")
    group = lax.div(energy, jnp.int32(GROUP))
    seat = lax.rem(energy, jnp.int32(GROUP))
    return energy, group, seat


def first_side(group):
    return 1 - 2 * lax.rem(group, jnp.int32(2))


def add_modes(total, sources, phonon_ref, offsets_ref, bose_ref):
    for mode in range(phonon_ref.shape[0]):
        shift, factor = offsets_ref[mode], bose_ref[mode]
        weights = []
        used = jnp.bool_(False)
        for _, distance in sources:
            below, above = distance == shift, distance == -shift
            weights.append(jnp.where(below, factor + 1.0, jnp.where(above, factor, 0.0)))
            used = jnp.logical_or(used, jnp.logical_or(below, above))

        @pl.when(used)
        def _(mode=mode, weights=weights):
            mixture = None
            for weight, (ref, _) in zip(weights, sources):
                term = weight * f32(ref[...])
                mixture = term if mixture is None else mixture + term
            matrix = phonon_ref[mode]
            total[...] += nt(bf(nn(matrix, bf(mixture))), matrix)


def to_seats(own_ref, first_ref, second_ref, phonon_ref, offsets_ref, bose_ref, *rest):
    *outs, total = rest
    _, group, seat = place()
    side = first_side(group)
    for j, out in enumerate(outs, 1):
        apart = jnp.bitwise_xor(seat, j) - seat
        sources = [
            (own_ref, apart),
            (first_ref, apart - GROUP * side),
            (second_ref, apart + GROUP * side),
        ]
        total[...] = jnp.zeros_like(total)
        add_modes(total, sources, phonon_ref, offsets_ref, bose_ref)
        out[...] = bf(total[...])


def dos(imag_ref, energy, energies):
    m = imag_ref.shape[0]
    rows = lax.broadcasted_iota(jnp.int32, (m, m), 0)
    columns = lax.broadcasted_iota(jnp.int32, (m, m), 1)
    diagonal = jnp.where(rows == columns, f32(imag_ref[...]), 0.0)
    position = jnp.full((1, m), f32(energy), jnp.float32)
    holes = 1.0 / (1.0 + jnp.exp(-((position + 0.5 - energies / 2) * 4.0 / energies)))
    return -holes * jnp.sum(diagonal, axis=0, keepdims=True)


def to_groups(energies, *refs):
    parts, (phonon_ref, offsets_ref, bose_ref) = refs[:GROUP], refs[GROUP : GROUP + 3]
    first_out, second_out, within_ref, sum_ref, total = refs[GROUP + 3 :]
    energy, group, seat = place()
    side = first_side(group)
    for out, toward in ((first_out, side), (second_out, -side)):
        sources = [
            (part, GROUP * toward + seat - jnp.bitwise_xor(seat, j)) for j, part in enumerate(parts)
        ]
        total[...] = jnp.zeros_like(total)
        add_modes(total, sources, phonon_ref, offsets_ref, bose_ref)
        out[...] = bf(total[...])
    within = jnp.zeros(within_ref.shape, jnp.float32)
    whole = jnp.zeros(sum_ref.shape, jnp.float32)
    for j, part in enumerate(parts):
        source = jnp.bitwise_xor(seat, j)
        terms = dos(part, energy - seat + source, energies)
        within = within + jnp.where(source <= seat, terms, 0.0)
        whole = whole + terms
    within_ref[...] = within
    sum_ref[...] = whole


def own_terms(*refs):
    parts = refs[: GROUP - 1]
    first_ref, second_ref, phonon_ref, offsets_ref, bose_ref, real_total, imag_total = refs[GROUP - 1 :]
    _, group, seat = place()
    side = first_side(group)
    real_total[...] = jnp.zeros_like(real_total)
    imag_total[...] = jnp.zeros_like(imag_total)
    column = [(first_ref, -GROUP * side), (second_ref, GROUP * side)]
    add_modes(real_total, column, phonon_ref, offsets_ref, bose_ref)
    sources = [(part, seat - jnp.bitwise_xor(seat, j)) for j, part in enumerate(parts, 1)]
    add_modes(imag_total, sources, phonon_ref, offsets_ref, bose_ref)


def last_sum(real_total, imag_total, a, b, c, first, second, out):
    m = real_total.shape[0]
    out[:, :m] = bf(real_total[...] + f32(a[...]) + f32(b[...]) + f32(c[...]))
    out[:, m:] = bf(imag_total[...] + f32(first[...]) + f32(second[...]))


def across_seats(value, j):
    energies = lax.axis_size("energy")
    return lax.ppermute(value, "energy", [(e, e ^ j) for e in range(energies)])


def across_groups(value, partner):
    groups = lax.axis_size("energy") // GROUP
    pairs = [(group, partner(group)) for group in range(groups)]
    return lax.ppermute(
        value,
        "energy",
        [(GROUP * a + i, GROUP * b + i) for a, b in pairs if 0 <= b < groups for i in range(GROUP)],
    )


def first_pair(group):
    return group ^ 1


def second_pair(group):
    return ((group + 1) ^ 1) - 1


def body(green_local, coupling, phonon_coupling, offsets, bose_factors):
    g = green_local[0]
    m = g.shape[0]
    energies = lax.axis_size("energy")
    half = jax.ShapeDtypeStruct((m, m), jnp.bfloat16)
    wide = jax.ShapeDtypeStruct((m, m), jnp.float32)
    line = jax.ShapeDtypeStruct((1, m), jnp.float32)
    total = [pltpu.VMEM((m, m), jnp.float32)]
    modes = [phonon_coupling, offsets, bose_factors]

    real, imag = greens_halves(g, coupling)
    first_real = across_groups(real, first_pair)
    second_real = across_groups(real, second_pair)
    imags = [imag] + [across_seats(imag, j) for j in range(1, GROUP)]

    sums = call(to_seats, [half] * (GROUP - 1), [real, first_real, second_real, *modes], total, 10, m)
    seat_terms = [across_seats(value, j) for j, value in enumerate(sums, 1)]

    first_out, second_out, within, group_sum = call(
        functools.partial(to_groups, energies), [half, half, line, line], [*imags, *modes], total, 12, m
    )
    first_term = across_groups(first_out, first_pair)
    second_term = across_groups(second_out, second_pair)

    real_total, imag_total = call(
        own_terms, [wide, wide], [*imags[1:], first_real, second_real, *modes], [], 6, m
    )

    group = place()[1]
    cumulative = within
    step = 1
    while step < energies // GROUP:
        received = across_groups(group_sum, lambda a, step=step: a ^ step)
        cumulative = cumulative + jnp.where(jnp.bitwise_and(group, step) > 0, received, 0.0)
        group_sum = group_sum + received
        step *= 2

    (sigma,) = call(
        last_sum,
        [jax.ShapeDtypeStruct(g.shape, jnp.bfloat16)],
        [real_total, imag_total, *seat_terms, first_term, second_term],
        [],
        0,
        m,
    )
    return sigma[None], cumulative


def solution(mesh):
    in_specs = (P("energy", "slab", None), P("slab", None), P(), P(), P())
    out_specs = (P("energy", "slab", None), P("energy", "slab"))
    return jax.shard_map(body, mesh=mesh, in_specs=in_specs, out_specs=out_specs, check_vma=False)
```

```python
import functools

import jax
import jax.numpy as jnp
from jax import lax
from jax.experimental import pallas as pl
from jax.experimental.pallas import tpu as pltpu
from jax.sharding import PartitionSpec as P

OMAX = 4
GROUP = OMAX
VMEM_LIMIT = 16 * 1024 * 1024

WHOLE = pl.BlockSpec(memory_space=pltpu.VMEM)
SCALARS = pl.BlockSpec(memory_space=pltpu.SMEM)


def nn(a, b):
    return lax.dot_general(a, b, (((1,), (0,)), ((), ())), preferred_element_type=jnp.float32)


def nt(a, b):
    return lax.dot_general(a, b, (((1,), (1,)), ((), ())), preferred_element_type=jnp.float32)


def tn(a, b):
    return lax.dot_general(a, b, (((0,), (0,)), ((), ())), preferred_element_type=jnp.float32)


def bf(value):
    return value.astype(jnp.bfloat16)


def f32(value):
    return value.astype(jnp.float32)


def call(kernel, outs, ins, scratch=(), flops=0):
    return pl.pallas_call(
        kernel,
        out_shape=outs,
        in_specs=[SCALARS if i.ndim == 1 else WHOLE for i in ins],
        out_specs=[WHOLE] * len(outs),
        scratch_shapes=scratch,
        compiler_params=pltpu.CompilerParams(vmem_limit_bytes=VMEM_LIMIT),
        cost_estimate=pl.CostEstimate(flops=flops, bytes_accessed=0, transcendentals=0),
    )(*ins)


def upper_term(link, block):
    m = link.shape[0]
    left = bf(nn(link, block))
    return bf(nt(left[:, :m], link)), bf(nt(left[:, m:], link))


def lower_term(link, block):
    m = link.shape[0]
    left = bf(tn(link, block))
    return bf(nn(left[:, :m], link)), bf(nn(left[:, m:], link))


def rotated(block):
    m = block.shape[0]
    return jnp.concatenate([-block[:, m:], block[:, :m]], axis=1)


def complex_product(first, second):
    m = first.shape[0]
    return nn(first[:, :m], second) + nn(first[:, m:], rotated(second))


def holes_at(energy, energies, shape):
    position = jnp.full(shape, f32(energy), jnp.float32)
    return 1.0 / (1.0 + jnp.exp(-((position + 0.5 - energies / 2) * 4.0 / energies)))


def hole_line(energies, out):
    out[...] = holes_at(lax.axis_index("energy"), energies, out.shape)


def diagonal_of(block_ref):
    m = block_ref.shape[0]
    tile = 128 if m % 128 == 0 else m
    rows = lax.broadcasted_iota(jnp.int32, (tile, tile), 0)
    columns = lax.broadcasted_iota(jnp.int32, (tile, tile), 1)
    parts = []
    for start in range(0, m, tile):
        block = f32(block_ref[start : start + tile, start : start + tile])
        parts.append(jnp.sum(jnp.where(rows == columns, block, 0.0), axis=0, keepdims=True))
    return jnp.concatenate(parts, axis=1)


def finish(g, dressed, holes_ref, real_ref, imag_ref, dos_ref):
    m = g.shape[0]
    greens = bf(f32(g) + complex_product(dressed, g) / m)
    real_ref[...] = greens[:, :m]
    imag_ref[...] = greens[:, m:]
    dos_ref[...] = -holes_ref[...] * diagonal_of(imag_ref)


def greens_of_pair(g_ref, other_ref, own_ref, below_ref, holes_ref, *rest):
    *outs, couple = rest
    m = own_ref.shape[0]
    slab = lax.axis_index("slab")

    @pl.when(slab == 0)
    def _():
        couple[:, :m], couple[:, m:] = upper_term(own_ref[...], other_ref[...])

    @pl.when(slab != 0)
    def _():
        couple[:, :m], couple[:, m:] = lower_term(below_ref[...], other_ref[...])

    g = g_ref[...]
    finish(g, bf(complex_product(g, couple[...])), holes_ref, *outs)


def greens_of_chain(g_ref, above_ref, lower_ref, own_ref, below_ref, holes_ref, *outs):
    up_real, up_imag = upper_term(own_ref[...], above_ref[...])
    low_real, low_imag = lower_term(below_ref[...], lower_ref[...])
    real = bf(f32(up_real) + f32(low_real))
    imag = bf(f32(up_imag) + f32(low_imag))
    g = g_ref[...]
    couple = jnp.concatenate([real, imag], axis=1)
    finish(g, bf(complex_product(g, couple)), holes_ref, *outs)


def greens_halves(g, coupling):
    m = g.shape[0]
    slabs = lax.axis_size("slab")
    half = jax.ShapeDtypeStruct((m, m), jnp.bfloat16)
    line = jax.ShapeDtypeStruct((1, m), jnp.float32)
    up = [(s, s + 1) for s in range(slabs - 1)]
    down = [(s + 1, s) for s in range(slabs - 1)]
    below = lax.ppermute(coupling, "slab", up)
    energies = lax.axis_size("energy")
    (holes,) = call(functools.partial(hole_line, energies), [line], [], flops=24 * m**3)
    if slabs == 2:
        other = lax.ppermute(g, "slab", up + down)
        couple = [pltpu.VMEM(g.shape, jnp.bfloat16)]
        ins = [g, other, coupling, below, holes]
        return call(greens_of_pair, [half, half, line], ins, couple)
    above = lax.ppermute(g, "slab", down)
    lower = lax.ppermute(g, "slab", up)
    ins = [g, above, lower, coupling, below, holes]
    return call(greens_of_chain, [half, half, line], ins)


def place():
    energy = lax.axis_index("energy")
    group = lax.div(energy, jnp.int32(GROUP))
    seat = lax.rem(energy, jnp.int32(GROUP))
    return energy, group, seat


def first_side(group):
    return 1 - 2 * lax.rem(group, jnp.int32(2))


def product(matrix, block, scale=None):
    left = nn(matrix, block)
    return nt(bf(left if scale is None else scale * left), matrix)


def mixed(first, first_weight, second, second_weight):
    return bf(first_weight * f32(first) + second_weight * f32(second))


def modes_of(offsets_ref):
    assert offsets_ref.shape == (3,)
    far = jnp.where(offsets_ref[1] == GROUP, 1, jnp.where(offsets_ref[2] == GROUP, 2, 0))
    return far, jnp.where(far == 0, 1, 0), jnp.where(far == 2, 1, 2)


def split_rows(line):
    high = bf(line)
    rest = line - f32(high)
    middle = bf(rest)
    low = bf(rest - f32(middle))
    rows = [f32(high), f32(middle), f32(low), jnp.zeros((13, line.shape[1]), jnp.float32)]
    return bf(jnp.concatenate(rows, axis=0))


def to_seats(own_ref, first_ref, second_ref, phonon_ref, offsets_ref, bose_ref, dos_ref, before_ref, *rest):
    *outs, bank, total = rest
    m = own_ref.shape[0]
    _, group, seat = place()
    side = first_side(group)
    bank[0] = own_ref[...]
    bank[1] = first_ref[...]
    bank[2] = second_ref[...]
    _, one, two = modes_of(offsets_ref)
    odd = jnp.where(lax.rem(offsets_ref[one], 2) == 1, one, two)
    left = one + two - odd

    def towards(j):
        apart = jnp.bitwise_xor(seat, j) - seat
        upward = apart > 0
        beside = jnp.where(upward == (side > 0), 1, 2)
        return jnp.abs(apart), upward, beside

    def single(j, mode):
        size, upward, beside = towards(j)
        shift, factor = offsets_ref[mode], bose_ref[mode]
        own = shift == size
        weight = jnp.where(own == upward, factor + 1.0, factor)
        return product(phonon_ref[mode], bank[jnp.where(own, 0, beside)], weight)

    for j in range(1, GROUP, 2):
        total[j // 2] = single(j, odd)

    @pl.when(lax.rem(offsets_ref[left], 2) == 0)
    def _():
        for j in range(1, GROUP, 2):
            outs[j - 1][:m] = bf(total[j // 2])
        factor = bose_ref[left]
        for j in range(2, GROUP, 2):
            _, upward, beside = towards(j)
            own_weight = jnp.where(upward, factor + 1.0, factor)
            beside_weight = jnp.where(upward, factor, factor + 1.0)
            block = mixed(bank[0], own_weight, bank[beside], beside_weight)
            outs[j - 1][:m] = bf(product(phonon_ref[left], block))

    @pl.when(lax.rem(offsets_ref[left], 2) == 1)
    def _():
        for j in range(1, GROUP, 2):
            outs[j - 1][:m] = bf(total[j // 2] + single(j, left))
        for j in range(2, GROUP, 2):
            outs[j - 1][:m] = jnp.zeros((m, m), jnp.bfloat16)

    for j, out in enumerate(outs, 1):
        counts = jnp.bitwise_xor(seat, j) > seat
        out[m:] = split_rows(before_ref[...] + jnp.where(counts, dos_ref[...], 0.0))


def to_groups(*refs):
    parts, (phonon_ref, offsets_ref, bose_ref) = refs[:GROUP], refs[GROUP : GROUP + 3]
    first_out, second_out, bank, total = refs[GROUP + 3 :]
    _, group, seat = place()
    upward = seat < GROUP // 2
    for j, part in enumerate(parts):
        bank[j] = part[...]
    far, _, _ = modes_of(offsets_ref)

    def gives(mode, up):
        shift, factor = offsets_ref[mode], bose_ref[mode]
        source = seat + jnp.where(up, GROUP - shift, shift - GROUP)
        inside = jnp.logical_and(source >= 0, source < GROUP)
        place_of = jnp.where(inside, jnp.bitwise_xor(seat, source), 0)
        return inside, place_of, jnp.where(up, factor + 1.0, factor)

    most = None
    for mode in range(phonon_ref.shape[0]):
        inside, place_of, weight = gives(mode, upward)
        whole = product(phonon_ref[mode], bank[place_of])
        total[mode] = whole
        term = jnp.where(inside, weight, 0.0) * whole
        most = term if most is None else most + term
    _, _, weight = gives(far, jnp.logical_not(upward))
    less = weight * total[far]
    total[0] = most
    total[1] = less
    for mode in range(phonon_ref.shape[0]):
        inside, place_of, weight = gives(mode, jnp.logical_not(upward))

        @pl.when(jnp.logical_and(mode != far, inside))
        def _(mode=mode, place_of=place_of, weight=weight):
            total[1] += product(phonon_ref[mode], bank[place_of], weight)

    most_first = upward == (first_side(group) > 0)
    first_out[...] = bf(total[jnp.where(most_first, 0, 1)])
    second_out[...] = bf(total[jnp.where(most_first, 1, 0)])


def column_terms(first_ref, second_ref, phonon_ref, offsets_ref, bose_ref, out):
    _, group, _ = place()
    side = first_side(group)
    far, _, _ = modes_of(offsets_ref)
    factor = bose_ref[far]
    first_weight = jnp.where(side > 0, factor, factor + 1.0)
    second_weight = jnp.where(side > 0, factor + 1.0, factor)
    block = mixed(first_ref[...], first_weight, second_ref[...], second_weight)
    out[...] = product(phonon_ref[far], block)


def group_terms(*refs):
    parts, (phonon_ref, offsets_ref, bose_ref, out, bank) = refs[: GROUP - 1], refs[GROUP - 1 :]
    _, _, seat = place()
    for j, part in enumerate(parts):
        bank[j] = part[...]
    _, *others = modes_of(offsets_ref)
    sum_of_modes = None
    for mode in others:
        shift, factor = offsets_ref[mode], bose_ref[mode]
        below, above = seat - shift, seat + shift
        has_below, has_above = below >= 0, above < GROUP
        first = jnp.where(has_below, jnp.bitwise_xor(seat, below) - 1, 0)
        second = jnp.where(has_above, jnp.bitwise_xor(seat, above) - 1, 0)
        block = mixed(
            bank[first],
            jnp.where(has_below, factor + 1.0, 0.0),
            bank[second],
            jnp.where(has_above, factor, 0.0),
        )
        term = product(phonon_ref[mode], block)
        sum_of_modes = term if sum_of_modes is None else sum_of_modes + term
    out[...] = sum_of_modes


def add_lines(a, b, out):
    out[...] = a[...] + b[...]


def column_sums(energies, first_ref, dos_ref, pair_out, dos_first_out):
    energy, group, _ = place()
    terms = -holes_at(energy + GROUP * first_side(group), energies, dos_ref.shape)
    terms = terms * diagonal_of(first_ref)
    dos_first_out[...] = terms
    pair_out[...] = terms + dos_ref[...]


def sums_before(*refs):
    *received, out = refs
    _, group, _ = place()
    line = jnp.zeros(out.shape, jnp.float32)
    for power, part in enumerate(received):
        line = line + jnp.where(jnp.bitwise_and(group, 1 << power) > 0, part[...], 0.0)
    out[...] = line


def last_sum(*refs):
    real_total, imag_total, first, second, before, dos = refs[:6]
    *seats, out, cumulative = refs[6:]
    m = real_total.shape[0]
    out[:, :m] = bf(real_total[...] + f32(first[...]) + f32(second[...]))
    imag = imag_total[...]
    line = before[...] + dos[...]
    for part in seats:
        imag = imag + f32(part[:m])
        line = line + jnp.sum(f32(part[m:]), axis=0, keepdims=True)
    out[:, m:] = bf(imag)
    cumulative[...] = line


def across_seats(value, j):
    energies = lax.axis_size("energy")
    return lax.ppermute(value, "energy", [(e, e ^ j) for e in range(energies)])


def across_groups(value, partner):
    groups = lax.axis_size("energy") // GROUP
    pairs = [(group, partner(group)) for group in range(groups)]
    return lax.ppermute(
        value,
        "energy",
        [(GROUP * a + i, GROUP * b + i) for a, b in pairs if 0 <= b < groups for i in range(GROUP)],
    )


def first_pair(group):
    return group ^ 1


def second_pair(group):
    return ((group + 1) ^ 1) - 1


def body(green_local, coupling, phonon_coupling, offsets, bose_factors):
    g = green_local[0]
    m = g.shape[0]
    groups = lax.axis_size("energy") // GROUP
    half = jax.ShapeDtypeStruct((m, m), jnp.bfloat16)
    taller = jax.ShapeDtypeStruct((m + 16, m), jnp.bfloat16)
    wide = jax.ShapeDtypeStruct((m, m), jnp.float32)
    line = jax.ShapeDtypeStruct((1, m), jnp.float32)
    modes = [phonon_coupling, offsets, bose_factors]

    def bank(blocks):
        return pltpu.VMEM((blocks, m, m), jnp.bfloat16)

    def totals(blocks):
        return pltpu.VMEM((blocks, m, m), jnp.float32)

    real, imag, dos = greens_halves(g, coupling)
    first_imag = across_groups(imag, first_pair)
    second_imag = across_groups(imag, second_pair)
    reals = [real] + [across_seats(real, j) for j in range(1, GROUP)]

    group_sum, dos_first = call(
        functools.partial(column_sums, lax.axis_size("energy")), [line, line], [first_imag, dos]
    )
    received = [dos_first]
    step = 2
    while step < groups:
        if step > 2:
            (group_sum,) = call(add_lines, [line], [group_sum, received[-1]])
        received.append(across_groups(group_sum, lambda a, step=step: a ^ step))
        step *= 2
    (imag_total,) = call(column_terms, [wide], [first_imag, second_imag, *modes])
    (before,) = call(sums_before, [line], received)

    sums = call(
        to_seats,
        [taller] * (GROUP - 1),
        [imag, first_imag, second_imag, *modes, dos, before],
        [bank(3), totals(GROUP // 2)],
    )
    seat_terms = [across_seats(value, j) for j, value in enumerate(sums, 1)]

    reals[0], _ = lax.optimization_barrier((reals[0], sums[0]))
    first_out, second_out = call(
        to_groups, [half, half], [*reals, *modes], [bank(GROUP), totals(len(offsets))]
    )
    first_term = across_groups(first_out, first_pair)
    second_term = across_groups(second_out, second_pair)
    (real_total,) = call(group_terms, [wide], [*reals[1:], *modes], [bank(GROUP - 1)])

    sigma, cumulative = call(
        last_sum,
        [jax.ShapeDtypeStruct(g.shape, jnp.bfloat16), line],
        [real_total, imag_total, first_term, second_term, before, dos, *seat_terms],
    )
    return sigma[None], cumulative


def solution(mesh):
    in_specs = (P("energy", "slab", None), P("slab", None), P(), P(), P())
    out_specs = (P("energy", "slab", None), P("energy", "slab"))
    return jax.shard_map(body, mesh=mesh, in_specs=in_specs, out_specs=out_specs, check_vma=False)
```

```python
import functools

import jax
import jax.numpy as jnp
from jax import lax
from jax.experimental import pallas as pl
from jax.experimental.pallas import tpu as pltpu
from jax.sharding import PartitionSpec as P

OMAX = 4
GROUP = OMAX
EXTRA = 16
LANES = 128
VMEM_LIMIT = 16 * 1024 * 1024

WHOLE = pl.BlockSpec(memory_space=pltpu.VMEM)
SCALARS = pl.BlockSpec(memory_space=pltpu.SMEM)


def nn(a, b):
    return lax.dot_general(a, b, (((1,), (0,)), ((), ())), preferred_element_type=jnp.float32)


def nt(a, b):
    return lax.dot_general(a, b, (((1,), (1,)), ((), ())), preferred_element_type=jnp.float32)


def tn(a, b):
    return lax.dot_general(a, b, (((0,), (0,)), ((), ())), preferred_element_type=jnp.float32)


def bf(value):
    return value.astype(jnp.bfloat16)


def f32(value):
    return value.astype(jnp.float32)


def call(kernel, outs, ins, scratch=(), flops=0, aliases=None):
    return pl.pallas_call(
        kernel,
        out_shape=outs,
        in_specs=[SCALARS if i.ndim == 1 else WHOLE for i in ins],
        out_specs=[WHOLE] * len(outs),
        scratch_shapes=scratch,
        input_output_aliases=aliases or {},
        compiler_params=pltpu.CompilerParams(vmem_limit_bytes=VMEM_LIMIT),
        cost_estimate=pl.CostEstimate(flops=flops, bytes_accessed=0, transcendentals=0),
    )(*ins)


def upper_term(link, block):
    m = link.shape[0]
    left = bf(nn(link, block))
    return bf(nt(left[:, :m], link)), bf(nt(left[:, m:], link))


def lower_term(link, block):
    m = link.shape[0]
    left = bf(tn(link, block))
    return bf(nn(left[:, :m], link)), bf(nn(left[:, m:], link))


def rotated(block):
    m = block.shape[0]
    return jnp.concatenate([-block[:, m:], block[:, :m]], axis=1)


def complex_product(first, second):
    m = first.shape[0]
    return nn(first[:, :m], second) + nn(first[:, m:], rotated(second))


def holes_at(energy, energies, shape):
    position = jnp.full(shape, f32(energy), jnp.float32)
    return 1.0 / (1.0 + jnp.exp(-((position + 0.5 - energies / 2) * 4.0 / energies)))


def prepare(energies, offsets_ref, bose_ref, holes_out, places_out, factors_out):
    assert offsets_ref.shape == (3,)
    holes_out[...] = holes_at(lax.axis_index("energy"), energies, holes_out.shape)
    far = jnp.where(offsets_ref[1] == GROUP, 1, jnp.where(offsets_ref[2] == GROUP, 2, 0))
    one, two = jnp.where(far == 0, 1, 0), jnp.where(far == 2, 1, 2)
    odd = jnp.where(lax.rem(offsets_ref[one], 2) == 1, one, two)
    for row, mode in enumerate((far, odd, one + two - odd)):
        places_out[row : row + 1] = jnp.full((1, LANES), mode, jnp.int32)
        places_out[row + 3 : row + 4] = jnp.full((1, LANES), offsets_ref[mode], jnp.int32)
        factors_out[row : row + 1] = jnp.full((1, LANES), bose_ref[mode], jnp.float32)


def modes_of(phonon_ref, places_ref, factors_ref):
    return [(places_ref[row, 0], places_ref[row + 3, 0], factors_ref[row, 0]) for row in range(3)]


def diagonal_of(block_ref):
    m = block_ref.shape[0]
    tile = 128 if m % 128 == 0 else m
    rows = lax.broadcasted_iota(jnp.int32, (tile, tile), 0)
    columns = lax.broadcasted_iota(jnp.int32, (tile, tile), 1)
    parts = []
    for start in range(0, m, tile):
        block = f32(block_ref[start : start + tile, start : start + tile])
        parts.append(jnp.sum(jnp.where(rows == columns, block, 0.0), axis=0, keepdims=True))
    return jnp.concatenate(parts, axis=1)


def finish(g, dressed, holes_ref, real_ref, imag_ref, dos_ref):
    m = g.shape[0]
    greens = bf(f32(g) + complex_product(dressed, g) / m)
    real_ref[...] = greens[:, :m]
    imag_ref[...] = greens[:, m:]
    dos_ref[...] = -holes_ref[...] * diagonal_of(imag_ref)


def greens_of_pair(g_ref, other_ref, own_ref, below_ref, holes_ref, *rest):
    *outs, couple = rest
    m = own_ref.shape[0]
    slab = lax.axis_index("slab")

    @pl.when(slab == 0)
    def _():
        couple[:, :m], couple[:, m:] = upper_term(own_ref[...], other_ref[...])

    @pl.when(slab != 0)
    def _():
        couple[:, :m], couple[:, m:] = lower_term(below_ref[...], other_ref[...])

    g = g_ref[...]
    finish(g, bf(complex_product(g, couple[...])), holes_ref, *outs)


def greens_of_chain(g_ref, above_ref, lower_ref, own_ref, below_ref, holes_ref, *outs):
    up_real, up_imag = upper_term(own_ref[...], above_ref[...])
    low_real, low_imag = lower_term(below_ref[...], lower_ref[...])
    real = bf(f32(up_real) + f32(low_real))
    imag = bf(f32(up_imag) + f32(low_imag))
    g = g_ref[...]
    couple = jnp.concatenate([real, imag], axis=1)
    finish(g, bf(complex_product(g, couple)), holes_ref, *outs)


def greens_halves(g, coupling, offsets, bose_factors):
    m = g.shape[0]
    slabs = lax.axis_size("slab")
    half = jax.ShapeDtypeStruct((m, m), jnp.bfloat16)
    line = jax.ShapeDtypeStruct((1, m), jnp.float32)
    places = jax.ShapeDtypeStruct((8, LANES), jnp.int32)
    factors = jax.ShapeDtypeStruct((8, LANES), jnp.float32)
    up = [(s, s + 1) for s in range(slabs - 1)]
    down = [(s + 1, s) for s in range(slabs - 1)]
    below = lax.ppermute(coupling, "slab", up)
    energies = lax.axis_size("energy")
    holes, *table = call(
        functools.partial(prepare, energies),
        [line, places, factors],
        [offsets, bose_factors],
        flops=24 * m**3,
    )
    if slabs == 2:
        other = lax.ppermute(g, "slab", up + down)
        couple = [pltpu.VMEM(g.shape, jnp.bfloat16)]
        ins = [g, other, coupling, below, holes]
        return *call(greens_of_pair, [half, half, line], ins, couple), table
    above = lax.ppermute(g, "slab", down)
    lower = lax.ppermute(g, "slab", up)
    ins = [g, above, lower, coupling, below, holes]
    return *call(greens_of_chain, [half, half, line], ins), table


def place():
    energy = lax.axis_index("energy")
    group = lax.div(energy, jnp.int32(GROUP))
    seat = lax.rem(energy, jnp.int32(GROUP))
    return energy, group, seat


def first_side(group):
    return 1 - 2 * lax.rem(group, jnp.int32(2))


def product(matrix, block, scale=None):
    left = nn(matrix, block)
    return nt(bf(left if scale is None else scale * left), matrix)


def mixed(first, first_weight, second, second_weight):
    return bf(first_weight * f32(first) + second_weight * f32(second))


def split_rows(line):
    high = bf(line)
    rest = line - f32(high)
    middle = bf(rest)
    low = bf(rest - f32(middle))
    rows = [f32(high), f32(middle), f32(low), jnp.zeros((EXTRA - 3, line.shape[1]), jnp.float32)]
    return bf(jnp.concatenate(rows, axis=0))


def to_seats(own_ref, first_ref, second_ref, phonon_ref, places_ref, factors_ref, *rest):
    *outs, bank, total = rest
    m = own_ref.shape[0]
    _, group, seat = place()
    side = first_side(group)
    bank[0] = own_ref[...]
    bank[1] = first_ref[...]
    bank[2] = second_ref[...]
    _, odd, left = modes_of(phonon_ref, places_ref, factors_ref)

    def towards(j):
        apart = jnp.bitwise_xor(seat, j) - seat
        upward = apart > 0
        beside = jnp.where(upward == (side > 0), 1, 2)
        return jnp.abs(apart), upward, beside

    def odd_seats(mode):
        index, shift, factor = mode
        blocks, weights = [], []
        for j in range(1, GROUP, 2):
            size, upward, beside = towards(j)
            own = shift == size
            blocks.append(bank[jnp.where(own, 0, beside)])
            weights.append(jnp.where(own == upward, factor + 1.0, factor))
        matrix = phonon_ref[index]
        wide = nn(matrix, jnp.concatenate(blocks, axis=1))
        parts = [bf(w * wide[:, i * m : (i + 1) * m]) for i, w in enumerate(weights)]
        return nt(jnp.concatenate(parts, axis=0), matrix)

    total[...] = odd_seats(odd)
    index, shift, factor = left

    @pl.when(lax.rem(shift, 2) == 0)
    def _():
        for j in range(2, GROUP, 2):
            _, upward, beside = towards(j)
            own_weight = jnp.where(upward, factor + 1.0, factor)
            beside_weight = jnp.where(upward, factor, factor + 1.0)
            block = mixed(bank[0], own_weight, bank[beside], beside_weight)
            outs[j - 1][:m] = bf(product(phonon_ref[index], block))

    @pl.when(lax.rem(shift, 2) == 1)
    def _():
        total[...] += odd_seats(left)
        for j in range(2, GROUP, 2):
            outs[j - 1][:m] = jnp.zeros((m, m), jnp.bfloat16)

    for j in range(1, GROUP, 2):
        outs[j - 1][:m] = bf(total[j // 2 * m : (j // 2 + 1) * m])
        outs[j - 1][m:] = jnp.zeros((EXTRA, m), jnp.bfloat16)
    for j in range(2, GROUP, 2):
        outs[j - 1][m:] = jnp.zeros((EXTRA, m), jnp.bfloat16)


def with_lines(dos_ref, before_ref, *refs):
    m = dos_ref.shape[1]
    _, _, seat = place()
    for j, out in enumerate(refs[GROUP - 1 :], 1):
        counts = jnp.bitwise_xor(seat, j) > seat
        out[m:] = split_rows(before_ref[...] + jnp.where(counts, dos_ref[...], 0.0))


def to_groups(*refs):
    parts, (phonon_ref, places_ref, factors_ref) = refs[:GROUP], refs[GROUP : GROUP + 3]
    first_out, second_out, bank, total = refs[GROUP + 3 :]
    _, group, seat = place()
    upward = seat < GROUP // 2
    for j, part in enumerate(parts):
        bank[j] = part[...]
    modes = modes_of(phonon_ref, places_ref, factors_ref)

    def gives(shift, factor, up):
        source = seat + jnp.where(up, GROUP - shift, shift - GROUP)
        inside = jnp.logical_and(source >= 0, source < GROUP)
        place_of = jnp.where(inside, jnp.bitwise_xor(seat, source), 0)
        return inside, place_of, jnp.where(up, factor + 1.0, factor)

    most = less = None
    for index, shift, factor in modes:
        inside, place_of, weight = gives(shift, factor, upward)
        whole = product(phonon_ref[index], bank[place_of])
        term = jnp.where(inside, weight, 0.0) * whole
        if most is None:
            most, less = term, gives(shift, factor, jnp.logical_not(upward))[2] * whole
        else:
            most = most + term
    total[0] = most
    total[1] = less
    for index, shift, factor in modes[1:]:
        inside, place_of, weight = gives(shift, factor, jnp.logical_not(upward))

        @pl.when(inside)
        def _(index=index, place_of=place_of, weight=weight):
            total[1] += product(phonon_ref[index], bank[place_of], weight)

    most_first = upward == (first_side(group) > 0)
    first_out[...] = bf(total[jnp.where(most_first, 0, 1)])
    second_out[...] = bf(total[jnp.where(most_first, 1, 0)])


def column_terms(first_ref, second_ref, phonon_ref, places_ref, factors_ref, out):
    _, group, _ = place()
    side = first_side(group)
    (index, _, factor), _, _ = modes_of(phonon_ref, places_ref, factors_ref)
    first_weight = jnp.where(side > 0, factor, factor + 1.0)
    second_weight = jnp.where(side > 0, factor + 1.0, factor)
    block = mixed(first_ref[...], first_weight, second_ref[...], second_weight)
    out[...] = product(phonon_ref[index], block)


def group_terms(*refs):
    parts, (phonon_ref, places_ref, factors_ref, out, bank) = refs[: GROUP - 1], refs[GROUP - 1 :]
    _, _, seat = place()
    for j, part in enumerate(parts):
        bank[j] = part[...]
    sum_of_modes = None
    for index, shift, factor in modes_of(phonon_ref, places_ref, factors_ref)[1:]:
        below, above = seat - shift, seat + shift
        has_below, has_above = below >= 0, above < GROUP
        first = jnp.where(has_below, jnp.bitwise_xor(seat, below) - 1, 0)
        second = jnp.where(has_above, jnp.bitwise_xor(seat, above) - 1, 0)
        block = mixed(
            bank[first],
            jnp.where(has_below, factor + 1.0, 0.0),
            bank[second],
            jnp.where(has_above, factor, 0.0),
        )
        term = product(phonon_ref[index], block)
        sum_of_modes = term if sum_of_modes is None else sum_of_modes + term
    out[...] = sum_of_modes


def add_lines(a, b, out):
    out[...] = a[...] + b[...]


def column_sums(energies, first_ref, dos_ref, pair_out, dos_first_out):
    energy, group, _ = place()
    terms = -holes_at(energy + GROUP * first_side(group), energies, dos_ref.shape)
    terms = terms * diagonal_of(first_ref)
    dos_first_out[...] = terms
    pair_out[...] = terms + dos_ref[...]


def sums_before(*refs):
    *received, out = refs
    _, group, _ = place()
    line = jnp.zeros(out.shape, jnp.float32)
    for power, part in enumerate(received):
        line = line + jnp.where(jnp.bitwise_and(group, 1 << power) > 0, part[...], 0.0)
    out[...] = line


def last_sum(*refs):
    real_total, imag_total, first, second, before, dos = refs[:6]
    *seats, out, cumulative = refs[6:]
    m = real_total.shape[0]
    out[:, :m] = bf(real_total[...] + f32(first[...]) + f32(second[...]))
    imag = imag_total[...]
    line = before[...] + dos[...]
    for part in seats:
        imag = imag + f32(part[:m])
        line = line + jnp.sum(f32(part[m:]), axis=0, keepdims=True)
    out[:, m:] = bf(imag)
    cumulative[...] = line


def across_seats(value, j):
    energies = lax.axis_size("energy")
    return lax.ppermute(value, "energy", [(e, e ^ j) for e in range(energies)])


def across_groups(value, partner):
    groups = lax.axis_size("energy") // GROUP
    pairs = [(group, partner(group)) for group in range(groups)]
    return lax.ppermute(
        value,
        "energy",
        [(GROUP * a + i, GROUP * b + i) for a, b in pairs if 0 <= b < groups for i in range(GROUP)],
    )


def first_pair(group):
    return group ^ 1


def second_pair(group):
    return ((group + 1) ^ 1) - 1


def body(green_local, coupling, phonon_coupling, offsets, bose_factors):
    g = green_local[0]
    m = g.shape[0]
    groups = lax.axis_size("energy") // GROUP
    half = jax.ShapeDtypeStruct((m, m), jnp.bfloat16)
    taller = jax.ShapeDtypeStruct((m + 16, m), jnp.bfloat16)
    wide = jax.ShapeDtypeStruct((m, m), jnp.float32)
    line = jax.ShapeDtypeStruct((1, m), jnp.float32)

    def bank(blocks):
        return pltpu.VMEM((blocks, m, m), jnp.bfloat16)

    def totals(blocks):
        return pltpu.VMEM((blocks, m, m), jnp.float32)

    real, imag, dos, table = greens_halves(g, coupling, offsets, bose_factors)
    modes = [phonon_coupling, *table]
    first_imag = across_groups(imag, first_pair)
    second_imag = across_groups(imag, second_pair)
    reals = [real] + [across_seats(real, j) for j in range(1, GROUP)]

    first_imag, reals[-1] = lax.optimization_barrier((first_imag, reals[-1]))

    group_sum, dos_first = call(
        functools.partial(column_sums, lax.axis_size("energy")), [line, line], [first_imag, dos]
    )
    received = [dos_first]
    step = 2
    while step < groups:
        if step > 2:
            (group_sum,) = call(add_lines, [line], [group_sum, received[-1]])
        received.append(across_groups(group_sum, lambda a, step=step: a ^ step))
        step *= 2

    sums = call(
        to_seats,
        [taller] * (GROUP - 1),
        [imag, first_imag, second_imag, *modes],
        [bank(3), pltpu.VMEM((GROUP // 2 * m, m), jnp.float32)],
    )
    (imag_total,) = call(column_terms, [wide], [first_imag, second_imag, *modes])
    received[-1], imag_total = lax.optimization_barrier((received[-1], imag_total))
    (before,) = call(sums_before, [line], received)
    sums = call(
        with_lines,
        [taller] * (GROUP - 1),
        [dos, before, *sums],
        aliases={2 + i: i for i in range(GROUP - 1)},
    )
    seat_terms = [across_seats(value, j) for j, value in enumerate(sums, 1)]

    reals[0], _ = lax.optimization_barrier((reals[0], sums[0]))
    first_out, second_out = call(
        to_groups, [half, half], [*reals, *modes], [bank(GROUP), totals(2)]
    )
    first_term = across_groups(first_out, first_pair)
    second_term = across_groups(second_out, second_pair)
    (real_total,) = call(group_terms, [wide], [*reals[1:], *modes], [bank(GROUP - 1)])

    sigma, cumulative = call(
        last_sum,
        [jax.ShapeDtypeStruct(g.shape, jnp.bfloat16), line],
        [real_total, imag_total, first_term, second_term, before, dos, *seat_terms],
    )
    return sigma[None], cumulative


def solution(mesh):
    in_specs = (P("energy", "slab", None), P("slab", None), P(), P(), P())
    out_specs = (P("energy", "slab", None), P("energy", "slab"))
    return jax.shard_map(body, mesh=mesh, in_specs=in_specs, out_specs=out_specs, check_vma=False)
```

```python
import functools

import jax
import jax.numpy as jnp
from jax import lax
from jax.experimental import pallas as pl
from jax.experimental.pallas import tpu as pltpu
from jax.sharding import PartitionSpec as P

OMAX = 4
GROUP = OMAX
EXTRA = 16
LANES = 128
VMEM_LIMIT = 16 * 1024 * 1024

WHOLE = pl.BlockSpec(memory_space=pltpu.VMEM)
OUTSIDE = pl.BlockSpec(memory_space=pl.ANY)
SCALARS = pl.BlockSpec(memory_space=pltpu.SMEM)


def nn(a, b):
    return lax.dot_general(a, b, (((1,), (0,)), ((), ())), preferred_element_type=jnp.float32)


def nt(a, b):
    return lax.dot_general(a, b, (((1,), (1,)), ((), ())), preferred_element_type=jnp.float32)


def tn(a, b):
    return lax.dot_general(a, b, (((0,), (0,)), ((), ())), preferred_element_type=jnp.float32)


def bf(value):
    return value.astype(jnp.bfloat16)


def f32(value):
    return value.astype(jnp.float32)


def call(kernel, outs, ins, scratch=(), flops=0, aliases=None, outside=()):
    return pl.pallas_call(
        kernel,
        out_shape=outs,
        in_specs=[SCALARS if i.ndim == 1 else WHOLE for i in ins],
        out_specs=[OUTSIDE if o in outside else WHOLE for o in range(len(outs))],
        scratch_shapes=scratch,
        input_output_aliases=aliases or {},
        compiler_params=pltpu.CompilerParams(vmem_limit_bytes=VMEM_LIMIT),
        cost_estimate=pl.CostEstimate(flops=flops, bytes_accessed=0, transcendentals=0),
    )(*ins)


def upper_term(link, block):
    m = link.shape[0]
    left = bf(nn(link, block))
    return bf(nt(left[:, :m], link)), bf(nt(left[:, m:], link))


def lower_term(link, block):
    m = link.shape[0]
    left = bf(tn(link, block))
    return bf(nn(left[:, :m], link)), bf(nn(left[:, m:], link))


def rotated(block):
    m = block.shape[0]
    return jnp.concatenate([-block[:, m:], block[:, :m]], axis=1)


def complex_product(first, second):
    return nn(first, jnp.concatenate([second, rotated(second)], axis=0))


def holes_at(energy, energies, shape):
    position = jnp.full(shape, f32(energy), jnp.float32)
    return 1.0 / (1.0 + jnp.exp(-((position + 0.5 - energies / 2) * 4.0 / energies)))


def prepare(energies, offsets_ref, bose_ref, holes_out, places_out, factors_out):
    assert offsets_ref.shape == (3,)
    holes_out[...] = holes_at(lax.axis_index("energy"), energies, holes_out.shape)
    far = jnp.where(offsets_ref[1] == GROUP, 1, jnp.where(offsets_ref[2] == GROUP, 2, 0))
    one, two = jnp.where(far == 0, 1, 0), jnp.where(far == 2, 1, 2)
    odd = jnp.where(lax.rem(offsets_ref[one], 2) == 1, one, two)
    for row, mode in enumerate((far, odd, one + two - odd)):
        places_out[row : row + 1] = jnp.full((1, LANES), mode, jnp.int32)
        places_out[row + 3 : row + 4] = jnp.full((1, LANES), offsets_ref[mode], jnp.int32)
        factors_out[row : row + 1] = jnp.full((1, LANES), bose_ref[mode], jnp.float32)


def modes_of(phonon_ref, places_ref, factors_ref):
    return [(places_ref[row, 0], places_ref[row + 3, 0], factors_ref[row, 0]) for row in range(3)]


def diagonal_of(block_ref):
    m = block_ref.shape[0]
    tile = 128 if m % 128 == 0 else m
    rows = lax.broadcasted_iota(jnp.int32, (tile, tile), 0)
    columns = lax.broadcasted_iota(jnp.int32, (tile, tile), 1)
    parts = []
    for start in range(0, m, tile):
        block = f32(block_ref[start : start + tile, start : start + tile])
        parts.append(jnp.sum(jnp.where(rows == columns, block, 0.0), axis=0, keepdims=True))
    return jnp.concatenate(parts, axis=1)


def finish(g, dressed, holes_ref, real_ref, imag_ref, dos_ref):
    m = g.shape[0]
    greens = bf(f32(g) + complex_product(dressed, g) / m)
    real_ref[...] = greens[:, :m]
    imag_ref[...] = greens[:, m:]
    dos_ref[...] = -holes_ref[...] * diagonal_of(imag_ref)


def greens_of_pair(g_ref, other_ref, own_ref, below_ref, holes_ref, *rest):
    *outs, couple = rest
    m = own_ref.shape[0]
    slab = lax.axis_index("slab")

    @pl.when(slab == 0)
    def _():
        couple[:, :m], couple[:, m:] = upper_term(own_ref[...], other_ref[...])

    @pl.when(slab != 0)
    def _():
        couple[:, :m], couple[:, m:] = lower_term(below_ref[...], other_ref[...])

    g = g_ref[...]
    finish(g, bf(complex_product(g, couple[...])), holes_ref, *outs)


def greens_of_chain(g_ref, above_ref, lower_ref, own_ref, below_ref, holes_ref, *outs):
    up_real, up_imag = upper_term(own_ref[...], above_ref[...])
    low_real, low_imag = lower_term(below_ref[...], lower_ref[...])
    real = bf(f32(up_real) + f32(low_real))
    imag = bf(f32(up_imag) + f32(low_imag))
    g = g_ref[...]
    couple = jnp.concatenate([real, imag], axis=1)
    finish(g, bf(complex_product(g, couple)), holes_ref, *outs)


def greens_halves(g, coupling, offsets, bose_factors):
    m = g.shape[0]
    slabs = lax.axis_size("slab")
    half = jax.ShapeDtypeStruct((m, m), jnp.bfloat16)
    line = jax.ShapeDtypeStruct((1, m), jnp.float32)
    places = jax.ShapeDtypeStruct((8, LANES), jnp.int32)
    factors = jax.ShapeDtypeStruct((8, LANES), jnp.float32)
    up = [(s, s + 1) for s in range(slabs - 1)]
    down = [(s + 1, s) for s in range(slabs - 1)]
    below = lax.ppermute(coupling, "slab", up)
    energies = lax.axis_size("energy")
    holes, *table = call(
        functools.partial(prepare, energies),
        [line, places, factors],
        [offsets, bose_factors],
        flops=24 * m**3,
    )
    if slabs == 2:
        other = lax.ppermute(g, "slab", up + down)
        couple = [pltpu.VMEM(g.shape, jnp.bfloat16)]
        ins = [g, other, coupling, below, holes]
        return *call(greens_of_pair, [half, half, line], ins, couple), table
    above = lax.ppermute(g, "slab", down)
    lower = lax.ppermute(g, "slab", up)
    ins = [g, above, lower, coupling, below, holes]
    return *call(greens_of_chain, [half, half, line], ins), table


def place():
    energy = lax.axis_index("energy")
    group = lax.div(energy, jnp.int32(GROUP))
    seat = lax.rem(energy, jnp.int32(GROUP))
    return energy, group, seat


def first_side(group):
    return 1 - 2 * lax.rem(group, jnp.int32(2))


def product(matrix, block, scale=None):
    left = nn(matrix, block)
    return nt(bf(left if scale is None else scale * left), matrix)


def mixed(first, first_weight, second, second_weight):
    return bf(first_weight * f32(first) + second_weight * f32(second))


def split_rows(line):
    high = bf(line)
    rest = line - f32(high)
    middle = bf(rest)
    low = bf(rest - f32(middle))
    rows = [f32(high), f32(middle), f32(low), jnp.zeros((EXTRA - 3, line.shape[1]), jnp.float32)]
    return bf(jnp.concatenate(rows, axis=0))


def to_seats(own_ref, first_ref, second_ref, phonon_ref, places_ref, factors_ref, *rest):
    *outs, bank = rest
    m = own_ref.shape[0]
    _, group, seat = place()
    side = first_side(group)
    bank[0] = own_ref[...]
    bank[1] = first_ref[...]
    bank[2] = second_ref[...]
    _, odd, left = modes_of(phonon_ref, places_ref, factors_ref)

    def towards(j):
        apart = jnp.bitwise_xor(seat, j) - seat
        upward = apart > 0
        beside = jnp.where(upward == (side > 0), 1, 2)
        return jnp.abs(apart), upward, beside

    def odd_seats(mode):
        index, shift, factor = mode
        blocks, weights = [], []
        for j in range(1, GROUP, 2):
            size, upward, beside = towards(j)
            own = shift == size
            blocks.append(bank[jnp.where(own, 0, beside)])
            weights.append(jnp.where(own == upward, factor + 1.0, factor))
        matrix = phonon_ref[index]
        wide = nn(matrix, jnp.concatenate(blocks, axis=1))
        parts = [bf(w * wide[:, i * m : (i + 1) * m]) for i, w in enumerate(weights)]
        return nt(jnp.concatenate(parts, axis=0), matrix)

    def put(wide):
        for j in range(1, GROUP, 2):
            outs[j - 1][:m] = bf(wide[j // 2 * m : (j // 2 + 1) * m])

    index, shift, factor = left

    @pl.when(lax.rem(shift, 2) == 0)
    def _():
        wide = odd_seats(odd)
        for j in range(2, GROUP, 2):
            _, upward, beside = towards(j)
            own_weight = jnp.where(upward, factor + 1.0, factor)
            beside_weight = jnp.where(upward, factor, factor + 1.0)
            block = mixed(bank[0], own_weight, bank[beside], beside_weight)
            outs[j - 1][:m] = bf(product(phonon_ref[index], block))
        put(wide)

    @pl.when(lax.rem(shift, 2) == 1)
    def _():
        put(odd_seats(odd) + odd_seats(left))
        for j in range(2, GROUP, 2):
            outs[j - 1][:m] = jnp.zeros((m, m), jnp.bfloat16)

    for out in outs:
        out[m:] = jnp.zeros((EXTRA, m), jnp.bfloat16)


def with_lines(dos_ref, before_ref, *refs):
    m = dos_ref.shape[1]
    _, _, seat = place()
    for j, out in enumerate(refs[GROUP - 1 :], 1):
        counts = jnp.bitwise_xor(seat, j) > seat
        out[m:] = split_rows(before_ref[...] + jnp.where(counts, dos_ref[...], 0.0))


def to_groups(*refs):
    parts, (phonon_ref, places_ref, factors_ref) = refs[:GROUP], refs[GROUP : GROUP + 3]
    first_out, second_out, bank, total = refs[GROUP + 3 :]
    _, group, seat = place()
    upward = seat < GROUP // 2
    for j, part in enumerate(parts):
        bank[j] = part[...]
    modes = modes_of(phonon_ref, places_ref, factors_ref)

    def gives(shift, factor, up):
        source = seat + jnp.where(up, GROUP - shift, shift - GROUP)
        inside = jnp.logical_and(source >= 0, source < GROUP)
        place_of = jnp.where(inside, jnp.bitwise_xor(seat, source), 0)
        return inside, place_of, jnp.where(up, factor + 1.0, factor)

    most = less = None
    for index, shift, factor in modes:
        inside, place_of, weight = gives(shift, factor, upward)
        whole = product(phonon_ref[index], bank[place_of])
        term = jnp.where(inside, weight, 0.0) * whole
        if most is None:
            most, less = term, gives(shift, factor, jnp.logical_not(upward))[2] * whole
        else:
            most = most + term
    total[0] = most
    total[1] = less
    for index, shift, factor in modes[1:]:
        inside, place_of, weight = gives(shift, factor, jnp.logical_not(upward))

        @pl.when(inside)
        def _(index=index, place_of=place_of, weight=weight):
            total[1] += product(phonon_ref[index], bank[place_of], weight)

    most_first = upward == (first_side(group) > 0)
    first_out[...] = bf(total[jnp.where(most_first, 0, 1)])
    second_out[...] = bf(total[jnp.where(most_first, 1, 0)])


def column_terms(first_ref, second_ref, phonon_ref, places_ref, factors_ref, out):
    _, group, _ = place()
    side = first_side(group)
    (index, _, factor), _, _ = modes_of(phonon_ref, places_ref, factors_ref)
    first_weight = jnp.where(side > 0, factor, factor + 1.0)
    second_weight = jnp.where(side > 0, factor + 1.0, factor)
    block = mixed(first_ref[...], first_weight, second_ref[...], second_weight)
    out[...] = product(phonon_ref[index], block)


def group_terms(*refs):
    parts, (phonon_ref, places_ref, factors_ref, out, bank) = refs[: GROUP - 1], refs[GROUP - 1 :]
    _, _, seat = place()
    for j, part in enumerate(parts):
        bank[j] = part[...]
    sum_of_modes = None
    for index, shift, factor in modes_of(phonon_ref, places_ref, factors_ref)[1:]:
        below, above = seat - shift, seat + shift
        has_below, has_above = below >= 0, above < GROUP
        first = jnp.where(has_below, jnp.bitwise_xor(seat, below) - 1, 0)
        second = jnp.where(has_above, jnp.bitwise_xor(seat, above) - 1, 0)
        block = mixed(
            bank[first],
            jnp.where(has_below, factor + 1.0, 0.0),
            bank[second],
            jnp.where(has_above, factor, 0.0),
        )
        term = product(phonon_ref[index], block)
        sum_of_modes = term if sum_of_modes is None else sum_of_modes + term
    out[...] = sum_of_modes


def add_lines(a, b, out):
    out[...] = a[...] + b[...]


def column_sums(energies, first_ref, dos_ref, pair_out, dos_first_out):
    energy, group, _ = place()
    terms = -holes_at(energy + GROUP * first_side(group), energies, dos_ref.shape)
    terms = terms * diagonal_of(first_ref)
    dos_first_out[...] = terms
    pair_out[...] = terms + dos_ref[...]


def sums_before(*refs):
    *received, out = refs
    _, group, _ = place()
    line = jnp.zeros(out.shape, jnp.float32)
    for power, part in enumerate(received):
        line = line + jnp.where(jnp.bitwise_and(group, 1 << power) > 0, part[...], 0.0)
    out[...] = line


def last_sum(*refs):
    real_total, imag_total, first, second, before, dos = refs[:6]
    *seats, out, cumulative, held, line, sems, line_sem = refs[6:]
    m = real_total.shape[0]
    density = before[...] + dos[...]
    for part in seats:
        density = density + jnp.sum(f32(part[m:]), axis=0, keepdims=True)
    line[...] = density
    copies = [pltpu.make_async_copy(line, cumulative, line_sem)]
    copies[0].start()
    pieces = sems.shape[0]
    for piece in range(pieces):
        rows = pl.ds(piece * (m // pieces), m // pieces)
        held[rows, :m] = bf(real_total[rows] + f32(first[rows]) + f32(second[rows]))
        imag = imag_total[rows]
        for part in seats:
            imag = imag + f32(part[rows])
        held[rows, m:] = bf(imag)
        copies.append(pltpu.make_async_copy(held.at[rows], out.at[rows], sems.at[piece]))
        copies[-1].start()
    for copy in copies:
        copy.wait()


def across_seats(value, j):
    energies = lax.axis_size("energy")
    return lax.ppermute(value, "energy", [(e, e ^ j) for e in range(energies)])


def across_groups(value, partner):
    groups = lax.axis_size("energy") // GROUP
    pairs = [(group, partner(group)) for group in range(groups)]
    return lax.ppermute(
        value,
        "energy",
        [(GROUP * a + i, GROUP * b + i) for a, b in pairs if 0 <= b < groups for i in range(GROUP)],
    )


def first_pair(group):
    return group ^ 1


def second_pair(group):
    return ((group + 1) ^ 1) - 1


def body(green_local, coupling, phonon_coupling, offsets, bose_factors):
    g = green_local[0]
    m = g.shape[0]
    groups = lax.axis_size("energy") // GROUP
    half = jax.ShapeDtypeStruct((m, m), jnp.bfloat16)
    taller = jax.ShapeDtypeStruct((m + 16, m), jnp.bfloat16)
    wide = jax.ShapeDtypeStruct((m, m), jnp.float32)
    line = jax.ShapeDtypeStruct((1, m), jnp.float32)

    def bank(blocks):
        return pltpu.VMEM((blocks, m, m), jnp.bfloat16)

    def totals(blocks):
        return pltpu.VMEM((blocks, m, m), jnp.float32)

    real, imag, dos, table = greens_halves(g, coupling, offsets, bose_factors)
    modes = [phonon_coupling, *table]
    first_imag = across_groups(imag, first_pair)
    second_imag = across_groups(imag, second_pair)
    reals = [real] + [across_seats(real, j) for j in range(1, GROUP)]

    first_imag, reals[-1] = lax.optimization_barrier((first_imag, reals[-1]))

    group_sum, dos_first = call(
        functools.partial(column_sums, lax.axis_size("energy")), [line, line], [first_imag, dos]
    )
    received = [dos_first]
    step = 2
    while step < groups:
        if step > 2:
            (group_sum,) = call(add_lines, [line], [group_sum, received[-1]])
        received.append(across_groups(group_sum, lambda a, step=step: a ^ step))
        step *= 2

    sums = call(
        to_seats,
        [taller] * (GROUP - 1),
        [imag, first_imag, second_imag, *modes],
        [bank(3)],
    )
    (imag_total,) = call(column_terms, [wide], [first_imag, second_imag, *modes])
    (before,) = call(sums_before, [line], received)
    sums = call(
        with_lines,
        [taller] * (GROUP - 1),
        [dos, before, *sums],
        aliases={2 + i: i for i in range(GROUP - 1)},
    )
    seat_terms = [across_seats(value, j) for j, value in enumerate(sums, 1)]

    reals[0], _ = lax.optimization_barrier((reals[0], sums[0]))
    first_out, second_out = call(
        to_groups, [half, half], [*reals, *modes], [bank(GROUP), totals(2)]
    )
    first_term = across_groups(first_out, first_pair)
    second_term = across_groups(second_out, second_pair)
    (real_total,) = call(group_terms, [wide], [*reals[1:], *modes], [bank(GROUP - 1)])

    pieces = 4 if m % 64 == 0 else 1
    sigma, cumulative = call(
        last_sum,
        [jax.ShapeDtypeStruct(g.shape, jnp.bfloat16), line],
        [real_total, imag_total, first_term, second_term, before, dos, *seat_terms],
        [
            pltpu.VMEM(g.shape, jnp.bfloat16),
            pltpu.VMEM((1, m), jnp.float32),
            pltpu.SemaphoreType.DMA((pieces,)),
            pltpu.SemaphoreType.DMA,
        ],
        outside=(0, 1),
    )
    return sigma[None], cumulative


def solution(mesh):
    in_specs = (P("energy", "slab", None), P("slab", None), P(), P(), P())
    out_specs = (P("energy", "slab", None), P("energy", "slab"))
    return jax.shard_map(body, mesh=mesh, in_specs=in_specs, out_specs=out_specs, check_vma=False)
```

```python
import functools

import jax
import jax.numpy as jnp
from jax import lax
from jax.experimental import pallas as pl
from jax.experimental.pallas import tpu as pltpu
from jax.sharding import PartitionSpec as P

OMAX = 4
GROUP = OMAX
EXTRA = 16
EXTRA_C = 16
EXTRA_B = 16
LANES = 128
VMEM_LIMIT = 16 * 1024 * 1024

WHOLE = pl.BlockSpec(memory_space=pltpu.VMEM)
OUTSIDE = pl.BlockSpec(memory_space=pl.ANY)
SCALARS = pl.BlockSpec(memory_space=pltpu.SMEM)


def nn(a, b):
    return lax.dot_general(a, b, (((1,), (0,)), ((), ())), preferred_element_type=jnp.float32)


def nt(a, b):
    return lax.dot_general(a, b, (((1,), (1,)), ((), ())), preferred_element_type=jnp.float32)


def tn(a, b):
    return lax.dot_general(a, b, (((0,), (0,)), ((), ())), preferred_element_type=jnp.float32)


def bf(value):
    return value.astype(jnp.bfloat16)


def f32(value):
    return value.astype(jnp.float32)


def call(kernel, outs, ins, scratch=(), flops=0, aliases=None, outside=()):
    return pl.pallas_call(
        kernel,
        out_shape=outs,
        in_specs=[SCALARS if i.ndim == 1 else WHOLE for i in ins],
        out_specs=[OUTSIDE if o in outside else WHOLE for o in range(len(outs))],
        scratch_shapes=scratch,
        input_output_aliases=aliases or {},
        compiler_params=pltpu.CompilerParams(vmem_limit_bytes=VMEM_LIMIT),
        cost_estimate=pl.CostEstimate(flops=flops, bytes_accessed=0, transcendentals=0),
    )(*ins)


def upper_term(link, block):
    m = link.shape[0]
    left = bf(nn(link, block))
    return bf(nt(left[:, :m], link)), bf(nt(left[:, m:], link))


def lower_term(link, block):
    m = link.shape[0]
    left = bf(tn(link, block))
    return bf(nn(left[:, :m], link)), bf(nn(left[:, m:], link))


def rotated(block):
    m = block.shape[0]
    return jnp.concatenate([-block[:, m:], block[:, :m]], axis=1)


def complex_product(first, second):
    return nn(first, jnp.concatenate([second, rotated(second)], axis=0))


def holes_at(energy, energies, shape):
    position = jnp.full(shape, f32(energy), jnp.float32)
    return 1.0 / (1.0 + jnp.exp(-((position + 0.5 - energies / 2) * 4.0 / energies)))


def hole_line(energies, out):
    out[...] = holes_at(lax.axis_index("energy"), energies, out.shape)


def mode_table(offsets_ref, bose_ref, places_out, factors_out):
    assert offsets_ref.shape == (3,)
    far = jnp.where(offsets_ref[1] == GROUP, 1, jnp.where(offsets_ref[2] == GROUP, 2, 0))
    one, two = jnp.where(far == 0, 1, 0), jnp.where(far == 2, 1, 2)
    odd = jnp.where(lax.rem(offsets_ref[one], 2) == 1, one, two)
    for row, mode in enumerate((far, odd, one + two - odd)):
        places_out[row : row + 1] = jnp.full((1, LANES), mode, jnp.int32)
        places_out[row + 3 : row + 4] = jnp.full((1, LANES), offsets_ref[mode], jnp.int32)
        factors_out[row : row + 1] = jnp.full((1, LANES), bose_ref[mode], jnp.float32)


def modes_of(phonon_ref, places_ref, factors_ref):
    return [(places_ref[row, 0], places_ref[row + 3, 0], factors_ref[row, 0]) for row in range(3)]


def diagonal_of(block_ref):
    m = block_ref.shape[0]
    tile = 128 if m % 128 == 0 else m
    rows = lax.broadcasted_iota(jnp.int32, (tile, tile), 0)
    columns = lax.broadcasted_iota(jnp.int32, (tile, tile), 1)
    parts = []
    for start in range(0, m, tile):
        block = f32(block_ref[start : start + tile, start : start + tile])
        parts.append(jnp.sum(jnp.where(rows == columns, block, 0.0), axis=0, keepdims=True))
    return jnp.concatenate(parts, axis=1)


def finish(g, dressed, holes_ref, real_ref, imag_ref, dos_ref):
    m = g.shape[0]
    greens = bf(f32(g) + complex_product(dressed, g) / m)
    real_ref[...] = greens[:, :m]
    imag_ref[...] = greens[:, m:]
    dos_ref[...] = -holes_ref[...] * diagonal_of(imag_ref)


def greens_of_first(g_ref, other_ref, own_ref, holes_ref, *rest):
    *outs, couple = rest

    @pl.when(lax.axis_index("slab") == 0)
    def _():
        m = own_ref.shape[0]
        couple[:, :m], couple[:, m:] = upper_term(own_ref[...], other_ref[...])
        g = g_ref[...]
        finish(g, bf(complex_product(g, couple[...])), holes_ref, *outs)


def greens_of_second(g_ref, other_ref, below_ref, holes_ref, *rest):
    *outs, couple = rest[3:]

    @pl.when(lax.axis_index("slab") != 0)
    def _():
        m = below_ref.shape[0]
        couple[:, :m], couple[:, m:] = lower_term(below_ref[...], other_ref[...])
        g = g_ref[...]
        finish(g, bf(complex_product(g, couple[...])), holes_ref, *outs)


def greens_of_chain(g_ref, above_ref, lower_ref, own_ref, below_ref, holes_ref, *outs):
    up_real, up_imag = upper_term(own_ref[...], above_ref[...])
    low_real, low_imag = lower_term(below_ref[...], lower_ref[...])
    real = bf(f32(up_real) + f32(low_real))
    imag = bf(f32(up_imag) + f32(low_imag))
    g = g_ref[...]
    couple = jnp.concatenate([real, imag], axis=1)
    finish(g, bf(complex_product(g, couple)), holes_ref, *outs)


def greens_halves(g, coupling):
    m = g.shape[0]
    slabs = lax.axis_size("slab")
    half = jax.ShapeDtypeStruct((m, m), jnp.bfloat16)
    line = jax.ShapeDtypeStruct((1, m), jnp.float32)
    outs = [half, half, line]
    up = [(s, s + 1) for s in range(slabs - 1)]
    down = [(s + 1, s) for s in range(slabs - 1)]
    below = lax.ppermute(coupling, "slab", up)
    energies = lax.axis_size("energy")
    (holes,) = call(functools.partial(hole_line, energies), [line], [], flops=24 * m**3)
    if slabs == 2:
        other = lax.ppermute(g, "slab", up + down)
        couple = [pltpu.VMEM(g.shape, jnp.bfloat16)]
        first = call(greens_of_first, outs, [g, other, coupling, holes], couple)
        ins = [g, other, below, holes, *first]
        return call(greens_of_second, outs, ins, couple, aliases={4: 0, 5: 1, 6: 2})
    above = lax.ppermute(g, "slab", down)
    lower = lax.ppermute(g, "slab", up)
    return call(greens_of_chain, outs, [g, above, lower, coupling, below, holes])


def place():
    energy = lax.axis_index("energy")
    group = lax.div(energy, jnp.int32(GROUP))
    seat = lax.rem(energy, jnp.int32(GROUP))
    return energy, group, seat


def hops():
    bit = 2 - lax.rem(lax.axis_index("slab"), 2)
    return bit, (GROUP - 1) - bit


def first_side(group):
    return 1 - 2 * lax.rem(group, jnp.int32(2))


def product(matrix, block, scale=None):
    left = nn(matrix, block)
    return nt(bf(left if scale is None else scale * left), matrix)


def mixed(first, first_weight, second, second_weight):
    return bf(first_weight * f32(first) + second_weight * f32(second))


def split_rows(line):
    high = bf(line)
    rest = line - f32(high)
    middle = bf(rest)
    low = bf(rest - f32(middle))
    rows = [f32(high), f32(middle), f32(low), jnp.zeros((EXTRA - 3, line.shape[1]), jnp.float32)]
    return bf(jnp.concatenate(rows, axis=0))


def to_seats(own_ref, first_ref, second_ref, phonon_ref, places_ref, factors_ref, *rest):
    across, direct, merged, bank, sums = rest
    m = own_ref.shape[0]
    _, group, seat = place()
    side = first_side(group)
    bank[0] = own_ref[...]
    bank[1] = first_ref[...]
    bank[2] = second_ref[...]
    _, odd, left = modes_of(phonon_ref, places_ref, factors_ref)

    def towards(j):
        apart = jnp.bitwise_xor(seat, j) - seat
        upward = apart > 0
        beside = jnp.where(upward == (side > 0), 1, 2)
        return jnp.abs(apart), upward, beside

    def odd_seats(mode):
        index, shift, factor = mode
        blocks, weights = [], []
        for j in (1, 3):
            size, upward, beside = towards(j)
            own = shift == size
            blocks.append(bank[jnp.where(own, 0, beside)])
            weights.append(jnp.where(own == upward, factor + 1.0, factor))
        matrix = phonon_ref[index]
        wide = nn(matrix, jnp.concatenate(blocks, axis=1))
        parts = [bf(w * wide[:, i * m : (i + 1) * m]) for i, w in enumerate(weights)]
        return nt(jnp.concatenate(parts, axis=0), matrix)

    def put(wide):
        sums[0] = bf(wide[:m])
        across[:m] = bf(wide[m:])

    index, shift, factor = left

    @pl.when(lax.rem(shift, 2) == 0)
    def _():
        wide = odd_seats(odd)
        _, upward, beside = towards(2)
        own_weight = jnp.where(upward, factor + 1.0, factor)
        beside_weight = jnp.where(upward, factor, factor + 1.0)
        block = mixed(bank[0], own_weight, bank[beside], beside_weight)
        sums[1] = bf(product(phonon_ref[index], block))
        put(wide)

    @pl.when(lax.rem(shift, 2) == 1)
    def _():
        put(odd_seats(odd) + odd_seats(left))
        sums[1] = jnp.zeros((m, m), jnp.bfloat16)

    first, second = hops()
    direct[:m] = sums[first - 1]
    merged[:m] = sums[second - 1]
    for out in (across, direct, merged):
        out[m:] = jnp.zeros((out.shape[0] - m, m), jnp.bfloat16)


def with_lines(dos_ref, before_ref, *refs):
    m = dos_ref.shape[1]
    _, _, seat = place()
    first, second = hops()
    for out, j in zip(refs[3:], (GROUP - 1, first, second)):
        counts = jnp.bitwise_xor(seat, j) > seat
        out[m : m + EXTRA] = split_rows(
            before_ref[...] + jnp.where(counts, dos_ref[...], 0.0)
        )


def merge(received_ref, merged_ref, out):
    m = received_ref.shape[1]
    out[:m] = bf(f32(merged_ref[:m]) + f32(received_ref[:m]))
    lines = f32(merged_ref[m : m + EXTRA]) + f32(received_ref[m : m + EXTRA])
    out[m : m + EXTRA] = split_rows(jnp.sum(lines, axis=0, keepdims=True))


def to_groups(*refs):
    parts, (phonon_ref, places_ref, factors_ref) = refs[:GROUP], refs[GROUP : GROUP + 3]
    first_out, second_out, bank, total = refs[GROUP + 3 :]
    _, group, seat = place()
    upward = seat < GROUP // 2
    first, second = hops()
    for j, part in zip((0, first, second, GROUP - 1), parts):
        bank[j] = part[...]
    modes = modes_of(phonon_ref, places_ref, factors_ref)

    def gives(shift, factor, up):
        source = seat + jnp.where(up, GROUP - shift, shift - GROUP)
        inside = jnp.logical_and(source >= 0, source < GROUP)
        place_of = jnp.where(inside, jnp.bitwise_xor(seat, source), 0)
        return inside, place_of, jnp.where(up, factor + 1.0, factor)

    most = less = None
    for index, shift, factor in modes:
        inside, place_of, weight = gives(shift, factor, upward)
        whole = product(phonon_ref[index], bank[place_of])
        term = jnp.where(inside, weight, 0.0) * whole
        if most is None:
            most, less = term, gives(shift, factor, jnp.logical_not(upward))[2] * whole
        else:
            most = most + term
    total[0] = most
    total[1] = less
    for index, shift, factor in modes[1:]:
        inside, place_of, weight = gives(shift, factor, jnp.logical_not(upward))

        @pl.when(inside)
        def _(index=index, place_of=place_of, weight=weight):
            total[1] += product(phonon_ref[index], bank[place_of], weight)

    most_first = upward == (first_side(group) > 0)
    m = bank.shape[1]
    first_out[:m] = bf(total[jnp.where(most_first, 0, 1)])
    second_out[:m] = bf(total[jnp.where(most_first, 1, 0)])
    for out in (first_out, second_out) if first_out.shape[0] > m else ():
        out[m:] = jnp.zeros((out.shape[0] - m, m), jnp.bfloat16)


def column_terms(first_ref, second_ref, phonon_ref, places_ref, factors_ref, out):
    _, group, _ = place()
    side = first_side(group)
    (index, _, factor), _, _ = modes_of(phonon_ref, places_ref, factors_ref)
    first_weight = jnp.where(side > 0, factor, factor + 1.0)
    second_weight = jnp.where(side > 0, factor + 1.0, factor)
    block = mixed(first_ref[...], first_weight, second_ref[...], second_weight)
    out[...] = product(phonon_ref[index], block)


def group_terms(*refs):
    parts, (phonon_ref, places_ref, factors_ref, out, bank) = refs[: GROUP - 1], refs[GROUP - 1 :]
    _, _, seat = place()
    first, second = hops()
    for j, part in zip((first, second, GROUP - 1), parts):
        bank[j - 1] = part[...]
    sum_of_modes = None
    for index, shift, factor in modes_of(phonon_ref, places_ref, factors_ref)[1:]:
        below, above = seat - shift, seat + shift
        has_below, has_above = below >= 0, above < GROUP
        first = jnp.where(has_below, jnp.bitwise_xor(seat, below) - 1, 0)
        second = jnp.where(has_above, jnp.bitwise_xor(seat, above) - 1, 0)
        block = mixed(
            bank[first],
            jnp.where(has_below, factor + 1.0, 0.0),
            bank[second],
            jnp.where(has_above, factor, 0.0),
        )
        term = product(phonon_ref[index], block)
        sum_of_modes = term if sum_of_modes is None else sum_of_modes + term
    out[...] = sum_of_modes


def add_lines(a, b, out):
    out[...] = a[...] + b[...]


def column_sums(energies, first_ref, dos_ref, pair_out, dos_first_out):
    energy, group, _ = place()
    terms = -holes_at(energy + GROUP * first_side(group), energies, dos_ref.shape)
    terms = terms * diagonal_of(first_ref)
    dos_first_out[...] = terms
    pair_out[...] = terms + dos_ref[...]


def sums_before(*refs):
    *received, out = refs
    _, group, _ = place()
    line = jnp.zeros(out.shape, jnp.float32)
    for power, part in enumerate(received):
        line = line + jnp.where(jnp.bitwise_and(group, 1 << power) > 0, part[...], 0.0)
    out[...] = line


def last_sum(*refs):
    real_total, imag_total, first, second, before, dos = refs[:6]
    *seats, out, cumulative, held, line, sems, line_sem = refs[6:]
    m = real_total.shape[0]
    density = before[...] + dos[...]
    for part in seats:
        density = density + jnp.sum(f32(part[m : m + EXTRA]), axis=0, keepdims=True)
    line[...] = density
    copies = [pltpu.make_async_copy(line, cumulative, line_sem)]
    copies[0].start()
    pieces = sems.shape[0]
    for piece in range(pieces):
        rows = pl.ds(piece * (m // pieces), m // pieces)
        held[rows, :m] = bf(real_total[rows] + f32(first[rows]) + f32(second[rows]))
        imag = imag_total[rows]
        for part in seats:
            imag = imag + f32(part[rows])
        held[rows, m:] = bf(imag)
        copies.append(pltpu.make_async_copy(held.at[rows], out.at[rows], sems.at[piece]))
        copies[-1].start()
    for copy in copies:
        copy.wait()


def hop(value, second):
    energies, slabs = lax.axis_size("energy"), lax.axis_size("slab")
    bits = [2 - slab % 2 for slab in range(slabs)]
    if second:
        bits = [GROUP - 1 - bit for bit in bits]
    pairs = [
        (e * slabs + slab, (e ^ bit) * slabs + slab)
        for e in range(energies)
        for slab, bit in enumerate(bits)
    ]
    return lax.ppermute(value, ("energy", "slab"), pairs)


def across_groups(value, partner):
    groups = lax.axis_size("energy") // GROUP
    pairs = [(group, partner(group)) for group in range(groups)]
    return lax.ppermute(
        value,
        "energy",
        [(GROUP * a + i, GROUP * b + i) for a, b in pairs if 0 <= b < groups for i in range(GROUP)],
    )


def first_pair(group):
    return group ^ 1


def second_pair(group):
    return ((group + 1) ^ 1) - 1


def body(green_local, coupling, phonon_coupling, offsets, bose_factors):
    g = green_local[0]
    m = g.shape[0]
    groups = lax.axis_size("energy") // GROUP
    half = jax.ShapeDtypeStruct((m, m), jnp.bfloat16)
    taller = jax.ShapeDtypeStruct((m + 16, m), jnp.bfloat16)
    wide = jax.ShapeDtypeStruct((m, m), jnp.float32)
    line = jax.ShapeDtypeStruct((1, m), jnp.float32)

    def bank(blocks):
        return pltpu.VMEM((blocks, m, m), jnp.bfloat16)

    def totals(blocks):
        return pltpu.VMEM((blocks, m, m), jnp.float32)

    real, imag, dos = greens_halves(g, coupling)
    places = jax.ShapeDtypeStruct((8, LANES), jnp.int32)
    factors = jax.ShapeDtypeStruct((8, LANES), jnp.float32)
    table = call(mode_table, [places, factors], [offsets, bose_factors])
    modes = [phonon_coupling, *table]
    first_imag = across_groups(imag, first_pair)
    second_imag = across_groups(imag, second_pair)
    near = hop(real, False)
    reals = [real, near, hop(real, True), hop(near, True)]

    first_imag, reals[1], *table = lax.optimization_barrier((first_imag, reals[1], *table))
    modes = [phonon_coupling, *table]

    group_sum, dos_first = call(
        functools.partial(column_sums, lax.axis_size("energy")), [line, line], [first_imag, dos]
    )
    received = [dos_first]
    step = 2
    while step < groups:
        if step > 2:
            (group_sum,) = call(add_lines, [line], [group_sum, received[-1]])
        received.append(across_groups(group_sum, lambda a, step=step: a ^ step))
        step *= 2

    heights = (m + EXTRA, m + EXTRA + EXTRA_B, m + EXTRA)
    taller = [jax.ShapeDtypeStruct((h, m), jnp.bfloat16) for h in heights]
    second_imag, reals[2] = lax.optimization_barrier((second_imag, reals[2]))
    sums = call(
        to_seats,
        taller,
        [imag, first_imag, second_imag, *modes],
        [bank(3), bank(2)],
    )
    (imag_total,) = call(column_terms, [wide], [first_imag, second_imag, *modes])
    received[-1], reals[3], *sums = lax.optimization_barrier((received[-1], reals[3], *sums))
    (before,) = call(sums_before, [line], received)
    sums = call(with_lines, taller, [dos, before, *sums], aliases={2: 0, 3: 1, 4: 2})
    direct_term = hop(sums[1], False)
    (merged,) = call(merge, taller[2:], [hop(sums[0], False), sums[2]])
    seat_terms = [direct_term, hop(merged, True)]

    reals[0], _ = lax.optimization_barrier((reals[0], sums[0]))
    for_groups = jax.ShapeDtypeStruct((m + EXTRA_C, m), jnp.bfloat16)
    first_out, second_out = call(
        to_groups, [for_groups] * 2, [*reals, *modes], [bank(GROUP), totals(2)]
    )
    first_term = across_groups(first_out, first_pair)
    second_term = across_groups(second_out, second_pair)
    (real_total,) = call(group_terms, [wide], [*reals[1:], *modes], [bank(GROUP - 1)])

    pieces = 4 if m % 64 == 0 else 1
    sigma, cumulative = call(
        last_sum,
        [jax.ShapeDtypeStruct(g.shape, jnp.bfloat16), line],
        [real_total, imag_total, first_term, second_term, before, dos, *seat_terms],
        [
            pltpu.VMEM(g.shape, jnp.bfloat16),
            pltpu.VMEM((1, m), jnp.float32),
            pltpu.SemaphoreType.DMA((pieces,)),
            pltpu.SemaphoreType.DMA,
        ],
        outside=(0, 1),
    )
    return sigma[None], cumulative


def solution(mesh):
    in_specs = (P("energy", "slab", None), P("slab", None), P(), P(), P())
    out_specs = (P("energy", "slab", None), P("energy", "slab"))
    return jax.shard_map(body, mesh=mesh, in_specs=in_specs, out_specs=out_specs, check_vma=False)
```

```python
import functools

import jax
import jax.numpy as jnp
from jax import lax
from jax.experimental import pallas as pl
from jax.experimental.pallas import tpu as pltpu
from jax.sharding import PartitionSpec as P

OMAX = 4
GROUP = OMAX
EXTRA = 16
EXTRA_C = 16
EXTRA_B = 16
LANES = 128
VMEM_LIMIT = 16 * 1024 * 1024

WHOLE = pl.BlockSpec(memory_space=pltpu.VMEM)
OUTSIDE = pl.BlockSpec(memory_space=pl.ANY)
SCALARS = pl.BlockSpec(memory_space=pltpu.SMEM)


def nn(a, b):
    return lax.dot_general(a, b, (((1,), (0,)), ((), ())), preferred_element_type=jnp.float32)


def nt(a, b):
    return lax.dot_general(a, b, (((1,), (1,)), ((), ())), preferred_element_type=jnp.float32)


def tn(a, b):
    return lax.dot_general(a, b, (((0,), (0,)), ((), ())), preferred_element_type=jnp.float32)


def bf(value):
    return value.astype(jnp.bfloat16)


def f32(value):
    return value.astype(jnp.float32)


def call(kernel, outs, ins, scratch=(), flops=0, aliases=None, outside=()):
    return pl.pallas_call(
        kernel,
        out_shape=outs,
        in_specs=[SCALARS if i.ndim == 1 else WHOLE for i in ins],
        out_specs=[OUTSIDE if o in outside else WHOLE for o in range(len(outs))],
        scratch_shapes=scratch,
        input_output_aliases=aliases or {},
        compiler_params=pltpu.CompilerParams(vmem_limit_bytes=VMEM_LIMIT),
        cost_estimate=pl.CostEstimate(flops=flops, bytes_accessed=0, transcendentals=0),
    )(*ins)


def upper_term(link, block):
    m = link.shape[0]
    left = bf(nn(link, block))
    return bf(nt(left[:, :m], link)), bf(nt(left[:, m:], link))


def lower_term(link, block):
    m = link.shape[0]
    left = bf(tn(link, block))
    return bf(nn(left[:, :m], link)), bf(nn(left[:, m:], link))


def rotated(block):
    m = block.shape[0]
    return jnp.concatenate([-block[:, m:], block[:, :m]], axis=1)


def complex_product(first, second):
    return nn(first, jnp.concatenate([second, rotated(second)], axis=0))


def holes_at(energy, energies, shape):
    position = jnp.full(shape, f32(energy), jnp.float32)
    return 1.0 / (1.0 + jnp.exp(-((position + 0.5 - energies / 2) * 4.0 / energies)))


def hole_line(energies, out):
    out[...] = holes_at(lax.axis_index("energy"), energies, out.shape)


def mode_table(offsets_ref, bose_ref, places_out, factors_out):
    assert offsets_ref.shape == (3,)
    far = jnp.where(offsets_ref[1] == GROUP, 1, jnp.where(offsets_ref[2] == GROUP, 2, 0))
    one, two = jnp.where(far == 0, 1, 0), jnp.where(far == 2, 1, 2)
    odd = jnp.where(lax.rem(offsets_ref[one], 2) == 1, one, two)
    for row, mode in enumerate((far, odd, one + two - odd)):
        places_out[row : row + 1] = jnp.full((1, LANES), mode, jnp.int32)
        places_out[row + 3 : row + 4] = jnp.full((1, LANES), offsets_ref[mode], jnp.int32)
        factors_out[row : row + 1] = jnp.full((1, LANES), bose_ref[mode], jnp.float32)


def modes_of(phonon_ref, places_ref, factors_ref):
    return [(places_ref[row, 0], places_ref[row + 3, 0], factors_ref[row, 0]) for row in range(3)]


def diagonal_of(block_ref):
    m = block_ref.shape[0]
    tile = 128 if m % 128 == 0 else m
    rows = lax.broadcasted_iota(jnp.int32, (tile, tile), 0)
    columns = lax.broadcasted_iota(jnp.int32, (tile, tile), 1)
    parts = []
    for start in range(0, m, tile):
        block = f32(block_ref[start : start + tile, start : start + tile])
        parts.append(jnp.sum(jnp.where(rows == columns, block, 0.0), axis=0, keepdims=True))
    return jnp.concatenate(parts, axis=1)


def finish(g, dressed, holes_ref, real_ref, imag_ref, dos_ref):
    m = g.shape[0]
    greens = bf(f32(g) + complex_product(dressed, g) / m)
    real_ref[...] = greens[:, :m]
    imag_ref[...] = greens[:, m:]
    dos_ref[...] = -holes_ref[...] * diagonal_of(imag_ref)


def greens_of_first(g_ref, other_ref, own_ref, holes_ref, *rest):
    *outs, couple = rest

    @pl.when(lax.axis_index("slab") == 0)
    def _():
        m = own_ref.shape[0]
        couple[:, :m], couple[:, m:] = upper_term(own_ref[...], other_ref[...])
        g = g_ref[...]
        finish(g, bf(complex_product(g, couple[...])), holes_ref, *outs)


def greens_of_second(g_ref, other_ref, below_ref, holes_ref, *rest):
    kept, (*outs, couple) = rest[:3], rest[3:]

    @pl.when(lax.axis_index("slab") == 0)
    def _():
        for out, value in zip(outs, kept):
            out[...] = value[...]

    @pl.when(lax.axis_index("slab") != 0)
    def _():
        m = below_ref.shape[0]
        couple[:, :m], couple[:, m:] = lower_term(below_ref[...], other_ref[...])
        g = g_ref[...]
        finish(g, bf(complex_product(g, couple[...])), holes_ref, *outs)


def greens_of_chain(g_ref, above_ref, lower_ref, own_ref, below_ref, holes_ref, *outs):
    up_real, up_imag = upper_term(own_ref[...], above_ref[...])
    low_real, low_imag = lower_term(below_ref[...], lower_ref[...])
    real = bf(f32(up_real) + f32(low_real))
    imag = bf(f32(up_imag) + f32(low_imag))
    g = g_ref[...]
    couple = jnp.concatenate([real, imag], axis=1)
    finish(g, bf(complex_product(g, couple)), holes_ref, *outs)


def greens_halves(g, coupling):
    m = g.shape[0]
    slabs = lax.axis_size("slab")
    half = jax.ShapeDtypeStruct((m, m), jnp.bfloat16)
    line = jax.ShapeDtypeStruct((1, m), jnp.float32)
    outs = [half, half, line]
    up = [(s, s + 1) for s in range(slabs - 1)]
    down = [(s + 1, s) for s in range(slabs - 1)]
    below = lax.ppermute(coupling, "slab", up)
    energies = lax.axis_size("energy")
    (holes,) = call(functools.partial(hole_line, energies), [line], [], flops=24 * m**3)
    if slabs == 2:
        other = lax.ppermute(g, "slab", up + down)
        couple = [pltpu.VMEM(g.shape, jnp.bfloat16)]
        first = call(greens_of_first, outs, [g, other, coupling, holes], couple)
        ins = [g, other, below, holes, *first]
        return call(greens_of_second, outs, ins, couple, aliases={4: 0, 5: 1, 6: 2})
    above = lax.ppermute(g, "slab", down)
    lower = lax.ppermute(g, "slab", up)
    return call(greens_of_chain, outs, [g, above, lower, coupling, below, holes])


def place():
    energy = lax.axis_index("energy")
    group = lax.div(energy, jnp.int32(GROUP))
    seat = lax.rem(energy, jnp.int32(GROUP))
    return energy, group, seat


def hops():
    bit = 2 - lax.rem(lax.axis_index("slab"), 2)
    return bit, (GROUP - 1) - bit


def first_side(group):
    return 1 - 2 * lax.rem(group, jnp.int32(2))


def product(matrix, block, scale=None):
    left = nn(matrix, block)
    return nt(bf(left if scale is None else scale * left), matrix)


def mixed(first, first_weight, second, second_weight):
    return bf(first_weight * f32(first) + second_weight * f32(second))


def split_rows(line):
    high = bf(line)
    rest = line - f32(high)
    middle = bf(rest)
    low = bf(rest - f32(middle))
    rows = [f32(high), f32(middle), f32(low), jnp.zeros((EXTRA - 3, line.shape[1]), jnp.float32)]
    return bf(jnp.concatenate(rows, axis=0))


def to_seats(own_ref, first_ref, second_ref, phonon_ref, places_ref, factors_ref, *rest):
    across, direct, merged, bank, sums = rest
    m = own_ref.shape[0]
    _, group, seat = place()
    side = first_side(group)
    bank[0] = own_ref[...]
    bank[1] = first_ref[...]
    bank[2] = second_ref[...]
    _, odd, left = modes_of(phonon_ref, places_ref, factors_ref)

    def towards(j):
        apart = jnp.bitwise_xor(seat, j) - seat
        upward = apart > 0
        beside = jnp.where(upward == (side > 0), 1, 2)
        return jnp.abs(apart), upward, beside

    def odd_seats(mode):
        index, shift, factor = mode
        blocks, weights = [], []
        for j in (1, 3):
            size, upward, beside = towards(j)
            own = shift == size
            blocks.append(bank[jnp.where(own, 0, beside)])
            weights.append(jnp.where(own == upward, factor + 1.0, factor))
        matrix = phonon_ref[index]
        wide = nn(matrix, jnp.concatenate(blocks, axis=1))
        parts = [bf(w * wide[:, i * m : (i + 1) * m]) for i, w in enumerate(weights)]
        return nt(jnp.concatenate(parts, axis=0), matrix)

    def put(wide):
        sums[0] = bf(wide[:m])
        across[:m] = bf(wide[m:])

    index, shift, factor = left

    @pl.when(lax.rem(shift, 2) == 0)
    def _():
        wide = odd_seats(odd)
        _, upward, beside = towards(2)
        own_weight = jnp.where(upward, factor + 1.0, factor)
        beside_weight = jnp.where(upward, factor, factor + 1.0)
        block = mixed(bank[0], own_weight, bank[beside], beside_weight)
        sums[1] = bf(product(phonon_ref[index], block))
        put(wide)

    @pl.when(lax.rem(shift, 2) == 1)
    def _():
        put(odd_seats(odd) + odd_seats(left))
        sums[1] = jnp.zeros((m, m), jnp.bfloat16)

    first, second = hops()
    direct[:m] = sums[first - 1]
    merged[:m] = sums[second - 1]
    for out in (across, direct, merged):
        out[m:] = jnp.zeros((out.shape[0] - m, m), jnp.bfloat16)


def with_lines(dos_ref, before_ref, *refs):
    m = dos_ref.shape[1]
    _, _, seat = place()
    first, second = hops()
    for kept, out, j in zip(refs[:3], refs[3:], (GROUP - 1, first, second)):
        out[...] = kept[...]
        counts = jnp.bitwise_xor(seat, j) > seat
        out[m : m + EXTRA] = split_rows(
            before_ref[...] + jnp.where(counts, dos_ref[...], 0.0)
        )


def merge(received_ref, merged_ref, out):
    m = received_ref.shape[1]
    out[:m] = bf(f32(merged_ref[:m]) + f32(received_ref[:m]))
    lines = f32(merged_ref[m : m + EXTRA]) + f32(received_ref[m : m + EXTRA])
    out[m : m + EXTRA] = split_rows(jnp.sum(lines, axis=0, keepdims=True))


def to_groups(*refs):
    parts, (phonon_ref, places_ref, factors_ref) = refs[:GROUP], refs[GROUP : GROUP + 3]
    first_out, second_out, bank, total = refs[GROUP + 3 :]
    _, group, seat = place()
    upward = seat < GROUP // 2
    first, second = hops()
    for j, part in zip((0, first, second, GROUP - 1), parts):
        bank[j] = part[...]
    modes = modes_of(phonon_ref, places_ref, factors_ref)

    def gives(shift, factor, up):
        source = seat + jnp.where(up, GROUP - shift, shift - GROUP)
        inside = jnp.logical_and(source >= 0, source < GROUP)
        place_of = jnp.where(inside, jnp.bitwise_xor(seat, source), 0)
        return inside, place_of, jnp.where(up, factor + 1.0, factor)

    most = less = None
    for index, shift, factor in modes:
        inside, place_of, weight = gives(shift, factor, upward)
        whole = product(phonon_ref[index], bank[place_of])
        term = jnp.where(inside, weight, 0.0) * whole
        if most is None:
            most, less = term, gives(shift, factor, jnp.logical_not(upward))[2] * whole
        else:
            most = most + term
    total[0] = most
    total[1] = less
    for index, shift, factor in modes[1:]:
        inside, place_of, weight = gives(shift, factor, jnp.logical_not(upward))

        @pl.when(inside)
        def _(index=index, place_of=place_of, weight=weight):
            total[1] += product(phonon_ref[index], bank[place_of], weight)

    most_first = upward == (first_side(group) > 0)
    m = bank.shape[1]
    first_out[:m] = bf(total[jnp.where(most_first, 0, 1)])
    second_out[:m] = bf(total[jnp.where(most_first, 1, 0)])
    for out in (first_out, second_out) if first_out.shape[0] > m else ():
        out[m:] = jnp.zeros((out.shape[0] - m, m), jnp.bfloat16)


def column_terms(first_ref, second_ref, phonon_ref, places_ref, factors_ref, out):
    _, group, _ = place()
    side = first_side(group)
    (index, _, factor), _, _ = modes_of(phonon_ref, places_ref, factors_ref)
    first_weight = jnp.where(side > 0, factor, factor + 1.0)
    second_weight = jnp.where(side > 0, factor + 1.0, factor)
    block = mixed(first_ref[...], first_weight, second_ref[...], second_weight)
    out[...] = product(phonon_ref[index], block)


def group_terms(*refs):
    parts, (phonon_ref, places_ref, factors_ref, out, bank) = refs[: GROUP - 1], refs[GROUP - 1 :]
    _, _, seat = place()
    first, second = hops()
    for j, part in zip((first, second, GROUP - 1), parts):
        bank[j - 1] = part[...]
    sum_of_modes = None
    for index, shift, factor in modes_of(phonon_ref, places_ref, factors_ref)[1:]:
        below, above = seat - shift, seat + shift
        has_below, has_above = below >= 0, above < GROUP
        first = jnp.where(has_below, jnp.bitwise_xor(seat, below) - 1, 0)
        second = jnp.where(has_above, jnp.bitwise_xor(seat, above) - 1, 0)
        block = mixed(
            bank[first],
            jnp.where(has_below, factor + 1.0, 0.0),
            bank[second],
            jnp.where(has_above, factor, 0.0),
        )
        term = product(phonon_ref[index], block)
        sum_of_modes = term if sum_of_modes is None else sum_of_modes + term
    out[...] = sum_of_modes


def add_lines(a, b, out):
    out[...] = a[...] + b[...]


def column_sums(energies, first_ref, dos_ref, pair_out, dos_first_out):
    energy, group, _ = place()
    terms = -holes_at(energy + GROUP * first_side(group), energies, dos_ref.shape)
    terms = terms * diagonal_of(first_ref)
    dos_first_out[...] = terms
    pair_out[...] = terms + dos_ref[...]


def sums_before(*refs):
    *received, out = refs
    _, group, _ = place()
    line = jnp.zeros(out.shape, jnp.float32)
    for power, part in enumerate(received):
        line = line + jnp.where(jnp.bitwise_and(group, 1 << power) > 0, part[...], 0.0)
    out[...] = line


def last_sum(*refs):
    real_total, imag_total, first, second, before, dos = refs[:6]
    *seats, out, cumulative, held, line, sems, line_sem = refs[6:]
    m = real_total.shape[0]
    density = before[...] + dos[...]
    for part in seats:
        density = density + jnp.sum(f32(part[m : m + EXTRA]), axis=0, keepdims=True)
    line[...] = density
    copies = [pltpu.make_async_copy(line, cumulative, line_sem)]
    copies[0].start()
    pieces = sems.shape[0]
    for piece in range(pieces):
        rows = pl.ds(piece * (m // pieces), m // pieces)
        held[rows, :m] = bf(real_total[rows] + f32(first[rows]) + f32(second[rows]))
        imag = imag_total[rows]
        for part in seats:
            imag = imag + f32(part[rows])
        held[rows, m:] = bf(imag)
        copies.append(pltpu.make_async_copy(held.at[rows], out.at[rows], sems.at[piece]))
        copies[-1].start()
    for copy in copies:
        copy.wait()


def hop(value, second):
    energies, slabs = lax.axis_size("energy"), lax.axis_size("slab")
    bits = [2 - slab % 2 for slab in range(slabs)]
    if second:
        bits = [GROUP - 1 - bit for bit in bits]
    pairs = [
        (e * slabs + slab, (e ^ bit) * slabs + slab)
        for e in range(energies)
        for slab, bit in enumerate(bits)
    ]
    return lax.ppermute(value, ("energy", "slab"), pairs)


def across_groups(value, partner):
    groups = lax.axis_size("energy") // GROUP
    pairs = [(group, partner(group)) for group in range(groups)]
    return lax.ppermute(
        value,
        "energy",
        [(GROUP * a + i, GROUP * b + i) for a, b in pairs if 0 <= b < groups for i in range(GROUP)],
    )


def first_pair(group):
    return group ^ 1


def second_pair(group):
    return ((group + 1) ^ 1) - 1


def body(green_local, coupling, phonon_coupling, offsets, bose_factors):
    g = green_local[0]
    m = g.shape[0]
    groups = lax.axis_size("energy") // GROUP
    half = jax.ShapeDtypeStruct((m, m), jnp.bfloat16)
    taller = jax.ShapeDtypeStruct((m + 16, m), jnp.bfloat16)
    wide = jax.ShapeDtypeStruct((m, m), jnp.float32)
    line = jax.ShapeDtypeStruct((1, m), jnp.float32)

    def bank(blocks):
        return pltpu.VMEM((blocks, m, m), jnp.bfloat16)

    def totals(blocks):
        return pltpu.VMEM((blocks, m, m), jnp.float32)

    real, imag, dos = greens_halves(g, coupling)
    places = jax.ShapeDtypeStruct((8, LANES), jnp.int32)
    factors = jax.ShapeDtypeStruct((8, LANES), jnp.float32)
    table = call(mode_table, [places, factors], [offsets, bose_factors])
    modes = [phonon_coupling, *table]
    first_imag = across_groups(imag, first_pair)
    second_imag = across_groups(imag, second_pair)
    near = hop(real, False)
    reals = [real, near, hop(real, True), hop(near, True)]

    first_imag, reals[1], *table = lax.optimization_barrier((first_imag, reals[1], *table))
    modes = [phonon_coupling, *table]

    group_sum, dos_first = call(
        functools.partial(column_sums, lax.axis_size("energy")), [line, line], [first_imag, dos]
    )
    received = [dos_first]
    step = 2
    while step < groups:
        if step > 2:
            (group_sum,) = call(add_lines, [line], [group_sum, received[-1]])
        received.append(across_groups(group_sum, lambda a, step=step: a ^ step))
        step *= 2

    heights = (m + EXTRA, m + EXTRA + EXTRA_B, m + EXTRA)
    taller = [jax.ShapeDtypeStruct((h, m), jnp.bfloat16) for h in heights]
    second_imag, reals[2] = lax.optimization_barrier((second_imag, reals[2]))
    sums = call(
        to_seats,
        taller,
        [imag, first_imag, second_imag, *modes],
        [bank(3), bank(2)],
    )
    (imag_total,) = call(column_terms, [wide], [first_imag, second_imag, *modes])
    received[-1], reals[3], *sums = lax.optimization_barrier((received[-1], reals[3], *sums))
    (before,) = call(sums_before, [line], received)
    sums = call(with_lines, taller, [dos, before, *sums], aliases={2: 0, 3: 1, 4: 2})
    direct_term = hop(sums[1], False)
    (merged,) = call(merge, taller[2:], [hop(sums[0], False), sums[2]])
    seat_terms = [direct_term, hop(merged, True)]

    reals[0], _ = lax.optimization_barrier((reals[0], sums[0]))
    for_groups = jax.ShapeDtypeStruct((m + EXTRA_C, m), jnp.bfloat16)
    first_out, second_out = call(
        to_groups, [for_groups] * 2, [*reals, *modes], [bank(GROUP), totals(2)]
    )
    first_term = across_groups(first_out, first_pair)
    second_term = across_groups(second_out, second_pair)
    (real_total,) = call(group_terms, [wide], [*reals[1:], *modes], [bank(GROUP - 1)])

    pieces = 4 if m % 64 == 0 else 1
    sigma, cumulative = call(
        last_sum,
        [jax.ShapeDtypeStruct(g.shape, jnp.bfloat16), line],
        [real_total, imag_total, first_term, second_term, before, dos, *seat_terms],
        [
            pltpu.VMEM(g.shape, jnp.bfloat16),
            pltpu.VMEM((1, m), jnp.float32),
            pltpu.SemaphoreType.DMA((pieces,)),
            pltpu.SemaphoreType.DMA,
        ],
        outside=(0, 1),
    )
    return sigma[None], cumulative


def solution(mesh):
    in_specs = (P("energy", "slab", None), P("slab", None), P(), P(), P())
    out_specs = (P("energy", "slab", None), P("energy", "slab"))
    return jax.shard_map(body, mesh=mesh, in_specs=in_specs, out_specs=out_specs, check_vma=False)
```

```python
import functools

import jax
import jax.numpy as jnp
from jax import lax
from jax.experimental import pallas as pl
from jax.experimental.pallas import tpu as pltpu
from jax.sharding import PartitionSpec as P

OMAX = 4
GROUP = OMAX
EXTRA = 16
EXTRA_C = 16
EXTRA_B = 16
LANES = 128
VMEM_LIMIT = 16 * 1024 * 1024

WHOLE = pl.BlockSpec(memory_space=pltpu.VMEM)
OUTSIDE = pl.BlockSpec(memory_space=pl.ANY)
SCALARS = pl.BlockSpec(memory_space=pltpu.SMEM)


def nn(a, b):
    return lax.dot_general(a, b, (((1,), (0,)), ((), ())), preferred_element_type=jnp.float32)


def nt(a, b):
    return lax.dot_general(a, b, (((1,), (1,)), ((), ())), preferred_element_type=jnp.float32)


def tn(a, b):
    return lax.dot_general(a, b, (((0,), (0,)), ((), ())), preferred_element_type=jnp.float32)


def bf(value):
    return value.astype(jnp.bfloat16)


def f32(value):
    return value.astype(jnp.float32)


def call(kernel, outs, ins, scratch=(), flops=0, aliases=None, outside=()):
    return pl.pallas_call(
        kernel,
        out_shape=outs,
        in_specs=[SCALARS if i.ndim == 1 else WHOLE for i in ins],
        out_specs=[OUTSIDE if o in outside else WHOLE for o in range(len(outs))],
        scratch_shapes=scratch,
        input_output_aliases=aliases or {},
        compiler_params=pltpu.CompilerParams(vmem_limit_bytes=VMEM_LIMIT),
        cost_estimate=pl.CostEstimate(flops=flops, bytes_accessed=0, transcendentals=0),
    )(*ins)


def upper_term(link, block):
    m = link.shape[0]
    left = bf(nn(link, block))
    return bf(nt(left[:, :m], link)), bf(nt(left[:, m:], link))


def lower_term(link, block):
    m = link.shape[0]
    left = bf(tn(link, block))
    return bf(nn(left[:, :m], link)), bf(nn(left[:, m:], link))


def rotated(block):
    m = block.shape[0]
    return jnp.concatenate([-block[:, m:], block[:, :m]], axis=1)


def complex_product(first, second):
    return nn(first, jnp.concatenate([second, rotated(second)], axis=0))


def holes_at(energy, energies, shape):
    position = jnp.full(shape, f32(energy), jnp.float32)
    return 1.0 / (1.0 + jnp.exp(-((position + 0.5 - energies / 2) * 4.0 / energies)))


def hole_line(energies, out):
    out[...] = holes_at(lax.axis_index("energy"), energies, out.shape)


def mode_table(offsets_ref, bose_ref, places_out, factors_out):
    assert offsets_ref.shape == (3,)
    far = jnp.where(offsets_ref[1] == GROUP, 1, jnp.where(offsets_ref[2] == GROUP, 2, 0))
    one, two = jnp.where(far == 0, 1, 0), jnp.where(far == 2, 1, 2)
    odd = jnp.where(lax.rem(offsets_ref[one], 2) == 1, one, two)
    for row, mode in enumerate((far, odd, one + two - odd)):
        places_out[row : row + 1] = jnp.full((1, LANES), mode, jnp.int32)
        places_out[row + 3 : row + 4] = jnp.full((1, LANES), offsets_ref[mode], jnp.int32)
        factors_out[row : row + 1] = jnp.full((1, LANES), bose_ref[mode], jnp.float32)


def modes_of(phonon_ref, places_ref, factors_ref):
    return [(places_ref[row, 0], places_ref[row + 3, 0], factors_ref[row, 0]) for row in range(3)]


def diagonal_of(block_ref):
    m = block_ref.shape[0]
    tile = 128 if m % 128 == 0 else m
    rows = lax.broadcasted_iota(jnp.int32, (tile, tile), 0)
    columns = lax.broadcasted_iota(jnp.int32, (tile, tile), 1)
    parts = []
    for start in range(0, m, tile):
        block = f32(block_ref[start : start + tile, start : start + tile])
        parts.append(jnp.sum(jnp.where(rows == columns, block, 0.0), axis=0, keepdims=True))
    return jnp.concatenate(parts, axis=1)


def finish(g, dressed, holes_ref, real_ref, imag_ref, dos_ref):
    m = g.shape[0]
    greens = bf(f32(g) + complex_product(dressed, g) / m)
    real_ref[...] = greens[:, :m]
    imag_ref[...] = greens[:, m:]
    dos_ref[...] = -holes_ref[...] * diagonal_of(imag_ref)


def greens_of_first(g_ref, other_ref, own_ref, holes_ref, *rest):
    *outs, couple = rest

    @pl.when(lax.axis_index("slab") == 0)
    def _():
        m = own_ref.shape[0]
        couple[:, :m], couple[:, m:] = upper_term(own_ref[...], other_ref[...])
        g = g_ref[...]
        finish(g, bf(complex_product(g, couple[...])), holes_ref, *outs)


def greens_of_second(g_ref, other_ref, below_ref, holes_ref, *rest):
    kept, (*outs, couple) = rest[:3], rest[3:]

    @pl.when(lax.axis_index("slab") == 0)
    def _():
        for out, value in zip(outs, kept):
            out[...] = value[...]

    @pl.when(lax.axis_index("slab") != 0)
    def _():
        m = below_ref.shape[0]
        couple[:, :m], couple[:, m:] = lower_term(below_ref[...], other_ref[...])
        g = g_ref[...]
        finish(g, bf(complex_product(g, couple[...])), holes_ref, *outs)


def greens_of_chain(g_ref, above_ref, lower_ref, own_ref, below_ref, holes_ref, *outs):
    up_real, up_imag = upper_term(own_ref[...], above_ref[...])
    low_real, low_imag = lower_term(below_ref[...], lower_ref[...])
    real = bf(f32(up_real) + f32(low_real))
    imag = bf(f32(up_imag) + f32(low_imag))
    g = g_ref[...]
    couple = jnp.concatenate([real, imag], axis=1)
    finish(g, bf(complex_product(g, couple)), holes_ref, *outs)


def greens_halves(g, coupling):
    m = g.shape[0]
    slabs = lax.axis_size("slab")
    half = jax.ShapeDtypeStruct((m, m), jnp.bfloat16)
    line = jax.ShapeDtypeStruct((1, m), jnp.float32)
    outs = [half, half, line]
    up = [(s, s + 1) for s in range(slabs - 1)]
    down = [(s + 1, s) for s in range(slabs - 1)]
    below = lax.ppermute(coupling, "slab", up)
    energies = lax.axis_size("energy")
    (holes,) = call(functools.partial(hole_line, energies), [line], [], flops=24 * m**3)
    if slabs == 2:
        other = lax.ppermute(g, "slab", up + down)
        couple = [pltpu.VMEM(g.shape, jnp.bfloat16)]
        first = call(greens_of_first, outs, [g, other, coupling, holes], couple)
        ins = [g, other, below, holes, *first]
        return call(greens_of_second, outs, ins, couple, aliases={4: 0, 5: 1, 6: 2})
    above = lax.ppermute(g, "slab", down)
    lower = lax.ppermute(g, "slab", up)
    return call(greens_of_chain, outs, [g, above, lower, coupling, below, holes])


def place():
    energy = lax.axis_index("energy")
    group = lax.div(energy, jnp.int32(GROUP))
    seat = lax.rem(energy, jnp.int32(GROUP))
    return energy, group, seat


def hops():
    bit = 2 - lax.rem(lax.axis_index("slab"), 2)
    return bit, (GROUP - 1) - bit


def first_side(group):
    return 1 - 2 * lax.rem(group, jnp.int32(2))


def product(matrix, block, scale=None):
    left = nn(matrix, block)
    return nt(bf(left if scale is None else scale * left), matrix)


def mixed(first, first_weight, second, second_weight):
    return bf(first_weight * f32(first) + second_weight * f32(second))


def split_rows(line):
    high = bf(line)
    rest = line - f32(high)
    middle = bf(rest)
    low = bf(rest - f32(middle))
    rows = [f32(high), f32(middle), f32(low), jnp.zeros((EXTRA - 3, line.shape[1]), jnp.float32)]
    return bf(jnp.concatenate(rows, axis=0))


def to_seats(own_ref, first_ref, second_ref, phonon_ref, places_ref, factors_ref, *rest):
    across, direct, merged, bank, sums = rest
    m = own_ref.shape[0]
    _, group, seat = place()
    side = first_side(group)
    bank[0] = own_ref[...]
    bank[1] = first_ref[...]
    bank[2] = second_ref[...]
    _, odd, left = modes_of(phonon_ref, places_ref, factors_ref)

    def towards(j):
        apart = jnp.bitwise_xor(seat, j) - seat
        upward = apart > 0
        beside = jnp.where(upward == (side > 0), 1, 2)
        return jnp.abs(apart), upward, beside

    def odd_seats(mode):
        index, shift, factor = mode
        blocks, weights = [], []
        for j in (1, 3):
            size, upward, beside = towards(j)
            own = shift == size
            blocks.append(bank[jnp.where(own, 0, beside)])
            weights.append(jnp.where(own == upward, factor + 1.0, factor))
        matrix = phonon_ref[index]
        wide = nn(matrix, jnp.concatenate(blocks, axis=1))
        parts = [bf(w * wide[:, i * m : (i + 1) * m]) for i, w in enumerate(weights)]
        return nt(jnp.concatenate(parts, axis=0), matrix)

    def put(wide):
        sums[0] = bf(wide[:m])
        across[:m] = bf(wide[m:])

    index, shift, factor = left

    @pl.when(lax.rem(shift, 2) == 0)
    def _():
        wide = odd_seats(odd)
        _, upward, beside = towards(2)
        own_weight = jnp.where(upward, factor + 1.0, factor)
        beside_weight = jnp.where(upward, factor, factor + 1.0)
        block = mixed(bank[0], own_weight, bank[beside], beside_weight)
        sums[1] = bf(product(phonon_ref[index], block))
        put(wide)

    @pl.when(lax.rem(shift, 2) == 1)
    def _():
        put(odd_seats(odd) + odd_seats(left))
        sums[1] = jnp.zeros((m, m), jnp.bfloat16)

    first, second = hops()
    direct[:m] = sums[first - 1]
    merged[:m] = sums[second - 1]


def with_lines(dos_ref, before_ref, *refs):
    m = dos_ref.shape[1]
    _, _, seat = place()
    first, second = hops()
    for kept, out, j in zip(refs[:3], refs[3:], (GROUP - 1, first, second)):
        out[:m] = kept[:m]
        counts = jnp.bitwise_xor(seat, j) > seat
        out[m : m + EXTRA] = split_rows(
            before_ref[...] + jnp.where(counts, dos_ref[...], 0.0)
        )
        if out.shape[0] > m + EXTRA:
            out[m + EXTRA :] = jnp.zeros((out.shape[0] - m - EXTRA, m), jnp.bfloat16)


def merge(received_ref, merged_ref, out):
    m = received_ref.shape[1]
    out[:m] = bf(f32(merged_ref[:m]) + f32(received_ref[:m]))
    lines = f32(merged_ref[m : m + EXTRA]) + f32(received_ref[m : m + EXTRA])
    out[m : m + EXTRA] = split_rows(jnp.sum(lines, axis=0, keepdims=True))


def to_groups(*refs):
    parts, (phonon_ref, places_ref, factors_ref) = refs[:GROUP], refs[GROUP : GROUP + 3]
    first_out, second_out, bank, total = refs[GROUP + 3 :]
    _, group, seat = place()
    upward = seat < GROUP // 2
    first, second = hops()
    for j, part in zip((0, first, second, GROUP - 1), parts):
        bank[j] = part[...]
    modes = modes_of(phonon_ref, places_ref, factors_ref)

    def gives(shift, factor, up):
        source = seat + jnp.where(up, GROUP - shift, shift - GROUP)
        inside = jnp.logical_and(source >= 0, source < GROUP)
        place_of = jnp.where(inside, jnp.bitwise_xor(seat, source), 0)
        return inside, place_of, jnp.where(up, factor + 1.0, factor)

    most = less = None
    for index, shift, factor in modes:
        inside, place_of, weight = gives(shift, factor, upward)
        whole = product(phonon_ref[index], bank[place_of])
        term = jnp.where(inside, weight, 0.0) * whole
        if most is None:
            most, less = term, gives(shift, factor, jnp.logical_not(upward))[2] * whole
        else:
            most = most + term
    total[0] = most
    total[1] = less
    for index, shift, factor in modes[1:]:
        inside, place_of, weight = gives(shift, factor, jnp.logical_not(upward))

        @pl.when(inside)
        def _(index=index, place_of=place_of, weight=weight):
            total[1] += product(phonon_ref[index], bank[place_of], weight)

    most_first = upward == (first_side(group) > 0)
    m = bank.shape[1]
    first_out[:m] = bf(total[jnp.where(most_first, 0, 1)])
    second_out[:m] = bf(total[jnp.where(most_first, 1, 0)])
    for out in (first_out, second_out) if first_out.shape[0] > m else ():
        out[m:] = jnp.zeros((out.shape[0] - m, m), jnp.bfloat16)


def column_terms(first_ref, second_ref, phonon_ref, places_ref, factors_ref, out):
    _, group, _ = place()
    side = first_side(group)
    (index, _, factor), _, _ = modes_of(phonon_ref, places_ref, factors_ref)
    first_weight = jnp.where(side > 0, factor, factor + 1.0)
    second_weight = jnp.where(side > 0, factor + 1.0, factor)
    block = mixed(first_ref[...], first_weight, second_ref[...], second_weight)
    out[...] = product(phonon_ref[index], block)


def group_terms(*refs):
    parts, (phonon_ref, places_ref, factors_ref, out, bank) = refs[: GROUP - 1], refs[GROUP - 1 :]
    _, _, seat = place()
    first, second = hops()
    for j, part in zip((first, second, GROUP - 1), parts):
        bank[j - 1] = part[...]
    sum_of_modes = None
    for index, shift, factor in modes_of(phonon_ref, places_ref, factors_ref)[1:]:
        below, above = seat - shift, seat + shift
        has_below, has_above = below >= 0, above < GROUP
        first = jnp.where(has_below, jnp.bitwise_xor(seat, below) - 1, 0)
        second = jnp.where(has_above, jnp.bitwise_xor(seat, above) - 1, 0)
        block = mixed(
            bank[first],
            jnp.where(has_below, factor + 1.0, 0.0),
            bank[second],
            jnp.where(has_above, factor, 0.0),
        )
        term = product(phonon_ref[index], block)
        sum_of_modes = term if sum_of_modes is None else sum_of_modes + term
    out[...] = sum_of_modes


def add_lines(a, b, out):
    out[...] = a[...] + b[...]


def column_sums(energies, first_ref, dos_ref, pair_out, dos_first_out):
    energy, group, _ = place()
    terms = -holes_at(energy + GROUP * first_side(group), energies, dos_ref.shape)
    terms = terms * diagonal_of(first_ref)
    dos_first_out[...] = terms
    pair_out[...] = terms + dos_ref[...]


def sums_before(*refs):
    *received, out = refs
    _, group, _ = place()
    line = jnp.zeros(out.shape, jnp.float32)
    for power, part in enumerate(received):
        line = line + jnp.where(jnp.bitwise_and(group, 1 << power) > 0, part[...], 0.0)
    out[...] = line


def last_sum(*refs):
    real_total, imag_total, first, second, before, dos = refs[:6]
    *seats, out, cumulative, held, line, sems, line_sem = refs[6:]
    m = real_total.shape[0]
    density = before[...] + dos[...]
    for part in seats:
        density = density + jnp.sum(f32(part[m : m + EXTRA]), axis=0, keepdims=True)
    line[...] = density
    copies = [pltpu.make_async_copy(line, cumulative, line_sem)]
    copies[0].start()
    pieces = sems.shape[0]
    for piece in range(pieces):
        rows = pl.ds(piece * (m // pieces), m // pieces)
        held[rows, :m] = bf(real_total[rows] + f32(first[rows]) + f32(second[rows]))
        imag = imag_total[rows]
        for part in seats:
            imag = imag + f32(part[rows])
        held[rows, m:] = bf(imag)
        copies.append(pltpu.make_async_copy(held.at[rows], out.at[rows], sems.at[piece]))
        copies[-1].start()
    for copy in copies:
        copy.wait()


def hop(value, second):
    energies, slabs = lax.axis_size("energy"), lax.axis_size("slab")
    bits = [2 - slab % 2 for slab in range(slabs)]
    if second:
        bits = [GROUP - 1 - bit for bit in bits]
    pairs = [
        (e * slabs + slab, (e ^ bit) * slabs + slab)
        for e in range(energies)
        for slab, bit in enumerate(bits)
    ]
    return lax.ppermute(value, ("energy", "slab"), pairs)


def across_groups(value, partner):
    groups = lax.axis_size("energy") // GROUP
    pairs = [(group, partner(group)) for group in range(groups)]
    return lax.ppermute(
        value,
        "energy",
        [(GROUP * a + i, GROUP * b + i) for a, b in pairs if 0 <= b < groups for i in range(GROUP)],
    )


def first_pair(group):
    return group ^ 1


def second_pair(group):
    return ((group + 1) ^ 1) - 1


def body(green_local, coupling, phonon_coupling, offsets, bose_factors):
    g = green_local[0]
    m = g.shape[0]
    groups = lax.axis_size("energy") // GROUP
    half = jax.ShapeDtypeStruct((m, m), jnp.bfloat16)
    taller = jax.ShapeDtypeStruct((m + 16, m), jnp.bfloat16)
    wide = jax.ShapeDtypeStruct((m, m), jnp.float32)
    line = jax.ShapeDtypeStruct((1, m), jnp.float32)

    def bank(blocks):
        return pltpu.VMEM((blocks, m, m), jnp.bfloat16)

    def totals(blocks):
        return pltpu.VMEM((blocks, m, m), jnp.float32)

    real, imag, dos = greens_halves(g, coupling)
    places = jax.ShapeDtypeStruct((8, LANES), jnp.int32)
    factors = jax.ShapeDtypeStruct((8, LANES), jnp.float32)
    table = call(mode_table, [places, factors], [offsets, bose_factors])
    modes = [phonon_coupling, *table]
    first_imag = across_groups(imag, first_pair)
    second_imag = across_groups(imag, second_pair)
    near = hop(real, False)
    reals = [real, near, hop(real, True), hop(near, True)]

    first_imag, reals[1], *table = lax.optimization_barrier((first_imag, reals[1], *table))
    modes = [phonon_coupling, *table]

    group_sum, dos_first = call(
        functools.partial(column_sums, lax.axis_size("energy")), [line, line], [first_imag, dos]
    )
    received = [dos_first]
    step = 2
    while step < groups:
        if step > 2:
            (group_sum,) = call(add_lines, [line], [group_sum, received[-1]])
        received.append(across_groups(group_sum, lambda a, step=step: a ^ step))
        step *= 2

    heights = (m + EXTRA, m + EXTRA + EXTRA_B, m + EXTRA)
    taller = [jax.ShapeDtypeStruct((h, m), jnp.bfloat16) for h in heights]
    second_imag, reals[2] = lax.optimization_barrier((second_imag, reals[2]))
    sums = call(
        to_seats,
        taller,
        [imag, first_imag, second_imag, *modes],
        [bank(3), bank(2)],
    )
    (imag_total,) = call(column_terms, [wide], [first_imag, second_imag, *modes])
    received[-1], reals[3], *sums = lax.optimization_barrier((received[-1], reals[3], *sums))
    (before,) = call(sums_before, [line], received)
    sums = call(with_lines, taller, [dos, before, *sums], aliases={2: 0, 3: 1, 4: 2})
    direct_term = hop(sums[1], False)
    (merged,) = call(merge, taller[2:], [hop(sums[0], False), sums[2]])
    seat_terms = [direct_term, hop(merged, True)]

    reals[0], _ = lax.optimization_barrier((reals[0], sums[0]))
    for_groups = jax.ShapeDtypeStruct((m + EXTRA_C, m), jnp.bfloat16)
    first_out, second_out = call(
        to_groups, [for_groups] * 2, [*reals, *modes], [bank(GROUP), totals(2)]
    )
    first_term = across_groups(first_out, first_pair)
    second_term = across_groups(second_out, second_pair)
    (real_total,) = call(group_terms, [wide], [*reals[1:], *modes], [bank(GROUP - 1)])

    pieces = 4 if m % 64 == 0 else 1
    sigma, cumulative = call(
        last_sum,
        [jax.ShapeDtypeStruct(g.shape, jnp.bfloat16), line],
        [real_total, imag_total, first_term, second_term, before, dos, *seat_terms],
        [
            pltpu.VMEM(g.shape, jnp.bfloat16),
            pltpu.VMEM((1, m), jnp.float32),
            pltpu.SemaphoreType.DMA((pieces,)),
            pltpu.SemaphoreType.DMA,
        ],
        outside=(0, 1),
    )
    return sigma[None], cumulative


def solution(mesh):
    in_specs = (P("energy", "slab", None), P("slab", None), P(), P(), P())
    out_specs = (P("energy", "slab", None), P("energy", "slab"))
    return jax.shard_map(body, mesh=mesh, in_specs=in_specs, out_specs=out_specs, check_vma=False)
```

```python
import functools

import jax
import jax.numpy as jnp
from jax import lax
from jax.experimental import pallas as pl
from jax.experimental.pallas import tpu as pltpu
from jax.sharding import PartitionSpec as P

OMAX = 4
GROUP = OMAX
EXTRA = 16
EXTRA_C = 16
EXTRA_B = 16
LANES = 128
VMEM_LIMIT = 16 * 1024 * 1024

WHOLE = pl.BlockSpec(memory_space=pltpu.VMEM)
OUTSIDE = pl.BlockSpec(memory_space=pl.ANY)
SCALARS = pl.BlockSpec(memory_space=pltpu.SMEM)


def nn(a, b):
    return lax.dot_general(a, b, (((1,), (0,)), ((), ())), preferred_element_type=jnp.float32)


def nt(a, b):
    return lax.dot_general(a, b, (((1,), (1,)), ((), ())), preferred_element_type=jnp.float32)


def tn(a, b):
    return lax.dot_general(a, b, (((0,), (0,)), ((), ())), preferred_element_type=jnp.float32)


def bf(value):
    return value.astype(jnp.bfloat16)


def f32(value):
    return value.astype(jnp.float32)


def call(kernel, outs, ins, scratch=(), flops=0, aliases=None, outside=()):
    return pl.pallas_call(
        kernel,
        out_shape=outs,
        in_specs=[SCALARS if i.ndim == 1 else WHOLE for i in ins],
        out_specs=[OUTSIDE if o in outside else WHOLE for o in range(len(outs))],
        scratch_shapes=scratch,
        input_output_aliases=aliases or {},
        compiler_params=pltpu.CompilerParams(vmem_limit_bytes=VMEM_LIMIT),
        cost_estimate=pl.CostEstimate(flops=flops, bytes_accessed=0, transcendentals=0),
    )(*ins)


def upper_term(link, block):
    m = link.shape[0]
    left = bf(nn(link, block))
    return bf(nt(left[:, :m], link)), bf(nt(left[:, m:], link))


def lower_term(link, block):
    m = link.shape[0]
    left = bf(tn(link, block))
    return bf(nn(left[:, :m], link)), bf(nn(left[:, m:], link))


def rotated(block):
    m = block.shape[0]
    return jnp.concatenate([-block[:, m:], block[:, :m]], axis=1)


def complex_product(first, second):
    return nn(first, jnp.concatenate([second, rotated(second)], axis=0))


def holes_at(energy, energies, shape):
    position = jnp.full(shape, f32(energy), jnp.float32)
    return 1.0 / (1.0 + jnp.exp(-((position + 0.5 - energies / 2) * 4.0 / energies)))


def hole_line(energies, out):
    out[...] = holes_at(lax.axis_index("energy"), energies, out.shape)


def mode_table(offsets_ref, bose_ref, places_out, factors_out):
    assert offsets_ref.shape == (3,)
    far = jnp.where(offsets_ref[1] == GROUP, 1, jnp.where(offsets_ref[2] == GROUP, 2, 0))
    one, two = jnp.where(far == 0, 1, 0), jnp.where(far == 2, 1, 2)
    odd = jnp.where(lax.rem(offsets_ref[one], 2) == 1, one, two)
    for row, mode in enumerate((far, odd, one + two - odd)):
        places_out[row : row + 1] = jnp.full((1, LANES), mode, jnp.int32)
        places_out[row + 3 : row + 4] = jnp.full((1, LANES), offsets_ref[mode], jnp.int32)
        factors_out[row : row + 1] = jnp.full((1, LANES), bose_ref[mode], jnp.float32)


def modes_of(phonon_ref, places_ref, factors_ref):
    return [(places_ref[row, 0], places_ref[row + 3, 0], factors_ref[row, 0]) for row in range(3)]


def diagonal_of(block_ref):
    m = block_ref.shape[0]
    tile = 128 if m % 128 == 0 else m
    rows = lax.broadcasted_iota(jnp.int32, (tile, tile), 0)
    columns = lax.broadcasted_iota(jnp.int32, (tile, tile), 1)
    parts = []
    for start in range(0, m, tile):
        block = f32(block_ref[start : start + tile, start : start + tile])
        parts.append(jnp.sum(jnp.where(rows == columns, block, 0.0), axis=0, keepdims=True))
    return jnp.concatenate(parts, axis=1)


def finish(g, dressed, holes_ref, real_ref, imag_ref, dos_ref):
    m = g.shape[0]
    greens = bf(f32(g) + complex_product(dressed, g) / m)
    real_ref[...] = greens[:, :m]
    imag_ref[...] = greens[:, m:]
    dos_ref[...] = -holes_ref[...] * diagonal_of(imag_ref)


def greens_of_first(g_ref, other_ref, own_ref, holes_ref, *rest):
    *outs, couple = rest

    @pl.when(lax.axis_index("slab") == 0)
    def _():
        m = own_ref.shape[0]
        couple[:, :m], couple[:, m:] = upper_term(own_ref[...], other_ref[...])
        g = g_ref[...]
        finish(g, bf(complex_product(g, couple[...])), holes_ref, *outs)


def greens_of_second(g_ref, other_ref, below_ref, holes_ref, *rest):
    kept, (*outs, couple) = rest[:3], rest[3:]

    @pl.when(lax.axis_index("slab") == 0)
    def _():
        for out, value in zip(outs, kept):
            out[...] = value[...]

    @pl.when(lax.axis_index("slab") != 0)
    def _():
        m = below_ref.shape[0]
        couple[:, :m], couple[:, m:] = lower_term(below_ref[...], other_ref[...])
        g = g_ref[...]
        finish(g, bf(complex_product(g, couple[...])), holes_ref, *outs)


def greens_of_chain(g_ref, above_ref, lower_ref, own_ref, below_ref, holes_ref, *outs):
    up_real, up_imag = upper_term(own_ref[...], above_ref[...])
    low_real, low_imag = lower_term(below_ref[...], lower_ref[...])
    real = bf(f32(up_real) + f32(low_real))
    imag = bf(f32(up_imag) + f32(low_imag))
    g = g_ref[...]
    couple = jnp.concatenate([real, imag], axis=1)
    finish(g, bf(complex_product(g, couple)), holes_ref, *outs)


def greens_halves(g, coupling):
    m = g.shape[0]
    slabs = lax.axis_size("slab")
    half = jax.ShapeDtypeStruct((m, m), jnp.bfloat16)
    line = jax.ShapeDtypeStruct((1, m), jnp.float32)
    outs = [half, half, line]
    up = [(s, s + 1) for s in range(slabs - 1)]
    down = [(s + 1, s) for s in range(slabs - 1)]
    below = lax.ppermute(coupling, "slab", up)
    energies = lax.axis_size("energy")
    (holes,) = call(functools.partial(hole_line, energies), [line], [], flops=24 * m**3)
    if slabs == 2:
        other = lax.ppermute(g, "slab", up + down)
        couple = [pltpu.VMEM(g.shape, jnp.bfloat16)]
        first = call(greens_of_first, outs, [g, other, coupling, holes], couple)
        ins = [g, other, below, holes, *first]
        return call(greens_of_second, outs, ins, couple, aliases={4: 0, 5: 1, 6: 2})
    above = lax.ppermute(g, "slab", down)
    lower = lax.ppermute(g, "slab", up)
    return call(greens_of_chain, outs, [g, above, lower, coupling, below, holes])


def place():
    energy = lax.axis_index("energy")
    group = lax.div(energy, jnp.int32(GROUP))
    seat = lax.rem(energy, jnp.int32(GROUP))
    return energy, group, seat


def hops():
    bit = 2 - lax.rem(lax.axis_index("slab"), 2)
    return bit, (GROUP - 1) - bit


def first_side(group):
    return 1 - 2 * lax.rem(group, jnp.int32(2))


def product(matrix, block, scale=None):
    left = nn(matrix, block)
    return nt(bf(left if scale is None else scale * left), matrix)


def mixed(first, first_weight, second, second_weight):
    return bf(first_weight * f32(first) + second_weight * f32(second))


def split_rows(line):
    high = bf(line)
    rest = line - f32(high)
    middle = bf(rest)
    low = bf(rest - f32(middle))
    rows = [f32(high), f32(middle), f32(low), jnp.zeros((EXTRA - 3, line.shape[1]), jnp.float32)]
    return bf(jnp.concatenate(rows, axis=0))


def to_seats(own_ref, first_ref, second_ref, phonon_ref, places_ref, factors_ref, *rest):
    across, direct, merged, bank, sums = rest
    m = own_ref.shape[0]
    _, group, seat = place()
    side = first_side(group)
    bank[0] = own_ref[...]
    bank[1] = first_ref[...]
    bank[2] = second_ref[...]
    _, odd, left = modes_of(phonon_ref, places_ref, factors_ref)

    def towards(j):
        apart = jnp.bitwise_xor(seat, j) - seat
        upward = apart > 0
        beside = jnp.where(upward == (side > 0), 1, 2)
        return jnp.abs(apart), upward, beside

    def odd_seats(mode):
        index, shift, factor = mode
        blocks, weights = [], []
        for j in (1, 3):
            size, upward, beside = towards(j)
            own = shift == size
            blocks.append(bank[jnp.where(own, 0, beside)])
            weights.append(jnp.where(own == upward, factor + 1.0, factor))
        matrix = phonon_ref[index]
        wide = nn(matrix, jnp.concatenate(blocks, axis=1))
        parts = [bf(w * wide[:, i * m : (i + 1) * m]) for i, w in enumerate(weights)]
        return nt(jnp.concatenate(parts, axis=0), matrix)

    def put(wide):
        sums[0] = bf(wide[:m])
        across[:m] = bf(wide[m:])

    index, shift, factor = left

    @pl.when(lax.rem(shift, 2) == 0)
    def _():
        wide = odd_seats(odd)
        _, upward, beside = towards(2)
        own_weight = jnp.where(upward, factor + 1.0, factor)
        beside_weight = jnp.where(upward, factor, factor + 1.0)
        block = mixed(bank[0], own_weight, bank[beside], beside_weight)
        sums[1] = bf(product(phonon_ref[index], block))
        put(wide)

    @pl.when(lax.rem(shift, 2) == 1)
    def _():
        put(odd_seats(odd) + odd_seats(left))
        sums[1] = jnp.zeros((m, m), jnp.bfloat16)

    first, second = hops()
    direct[:m] = sums[first - 1]
    merged[:m] = sums[second - 1]


def with_lines(dos_ref, before_ref, *refs):
    m = dos_ref.shape[1]
    _, _, seat = place()
    first, second = hops()
    for kept, out, j in zip(refs[:3], refs[3:], (GROUP - 1, first, second)):
        out[:m] = kept[:m]
        counts = jnp.bitwise_xor(seat, j) > seat
        out[m : m + EXTRA] = split_rows(
            before_ref[...] + jnp.where(counts, dos_ref[...], 0.0)
        )
        if out.shape[0] > m + EXTRA:
            out[m + EXTRA :] = jnp.zeros((out.shape[0] - m - EXTRA, m), jnp.bfloat16)


def merge(received_ref, merged_ref, out):
    m = received_ref.shape[1]
    out[:m] = bf(f32(merged_ref[:m]) + f32(received_ref[:m]))
    lines = f32(merged_ref[m : m + EXTRA]) + f32(received_ref[m : m + EXTRA])
    out[m : m + EXTRA] = split_rows(jnp.sum(lines, axis=0, keepdims=True))


def to_groups(*refs):
    parts, (phonon_ref, places_ref, factors_ref) = refs[:GROUP], refs[GROUP : GROUP + 3]
    first_out, second_out, bank, total = refs[GROUP + 3 :]
    _, group, seat = place()
    upward = seat < GROUP // 2
    first, second = hops()
    for j, part in zip((first, second, GROUP - 1), parts[1:]):
        bank[j - 1] = part[...]
    modes = modes_of(phonon_ref, places_ref, factors_ref)

    def gives(shift, factor, up):
        source = seat + jnp.where(up, GROUP - shift, shift - GROUP)
        inside = jnp.logical_and(source >= 0, source < GROUP)
        place_of = jnp.where(inside, jnp.bitwise_xor(seat, source) - 1, 0)
        return inside, place_of, jnp.where(up, factor + 1.0, factor)

    most = less = None
    for index, shift, factor in modes:
        inside, place_of, weight = gives(shift, factor, upward)
        block = parts[0][...] if most is None else bank[place_of]
        whole = product(phonon_ref[index], block)
        term = jnp.where(inside, weight, 0.0) * whole
        if most is None:
            most, less = term, gives(shift, factor, jnp.logical_not(upward))[2] * whole
        else:
            most = most + term
    total[0] = most
    total[1] = less
    for index, shift, factor in modes[1:]:
        inside, place_of, weight = gives(shift, factor, jnp.logical_not(upward))

        @pl.when(inside)
        def _(index=index, place_of=place_of, weight=weight):
            total[1] += product(phonon_ref[index], bank[place_of], weight)

    most_first = upward == (first_side(group) > 0)
    m = bank.shape[1]
    first_out[:m] = bf(total[jnp.where(most_first, 0, 1)])
    second_out[:m] = bf(total[jnp.where(most_first, 1, 0)])
    for out in (first_out, second_out) if first_out.shape[0] > m else ():
        out[m:] = jnp.zeros((out.shape[0] - m, m), jnp.bfloat16)


def column_terms(first_ref, second_ref, phonon_ref, places_ref, factors_ref, out):
    _, group, _ = place()
    side = first_side(group)
    (index, _, factor), _, _ = modes_of(phonon_ref, places_ref, factors_ref)
    first_weight = jnp.where(side > 0, factor, factor + 1.0)
    second_weight = jnp.where(side > 0, factor + 1.0, factor)
    block = mixed(first_ref[...], first_weight, second_ref[...], second_weight)
    out[...] = product(phonon_ref[index], block)


def group_terms(*refs):
    parts, (phonon_ref, places_ref, factors_ref, out, bank) = refs[: GROUP - 1], refs[GROUP - 1 :]
    _, _, seat = place()
    first, second = hops()
    for j, part in zip((first, second, GROUP - 1), parts):
        bank[j - 1] = part[...]
    sum_of_modes = None
    for index, shift, factor in modes_of(phonon_ref, places_ref, factors_ref)[1:]:
        below, above = seat - shift, seat + shift
        has_below, has_above = below >= 0, above < GROUP
        first = jnp.where(has_below, jnp.bitwise_xor(seat, below) - 1, 0)
        second = jnp.where(has_above, jnp.bitwise_xor(seat, above) - 1, 0)
        block = mixed(
            bank[first],
            jnp.where(has_below, factor + 1.0, 0.0),
            bank[second],
            jnp.where(has_above, factor, 0.0),
        )
        term = product(phonon_ref[index], block)
        sum_of_modes = term if sum_of_modes is None else sum_of_modes + term
    out[...] = sum_of_modes


def add_lines(a, b, out):
    out[...] = a[...] + b[...]


def column_sums(energies, first_ref, dos_ref, pair_out, dos_first_out):
    energy, group, _ = place()
    terms = -holes_at(energy + GROUP * first_side(group), energies, dos_ref.shape)
    terms = terms * diagonal_of(first_ref)
    dos_first_out[...] = terms
    pair_out[...] = terms + dos_ref[...]


def sums_before(*refs):
    *received, out = refs
    _, group, _ = place()
    line = jnp.zeros(out.shape, jnp.float32)
    for power, part in enumerate(received):
        line = line + jnp.where(jnp.bitwise_and(group, 1 << power) > 0, part[...], 0.0)
    out[...] = line


def last_sum(*refs):
    real_total, imag_total, first, second, before, dos = refs[:6]
    *seats, out, cumulative, held, line, sems, line_sem = refs[6:]
    m = real_total.shape[0]
    density = before[...] + dos[...]
    for part in seats:
        density = density + jnp.sum(f32(part[m : m + EXTRA]), axis=0, keepdims=True)
    line[...] = density
    copies = [pltpu.make_async_copy(line, cumulative, line_sem)]
    copies[0].start()
    pieces = sems.shape[0]
    for piece in range(pieces):
        rows = pl.ds(piece * (m // pieces), m // pieces)
        held[rows, :m] = bf(real_total[rows] + f32(first[rows]) + f32(second[rows]))
        imag = imag_total[rows]
        for part in seats:
            imag = imag + f32(part[rows])
        held[rows, m:] = bf(imag)
        copies.append(pltpu.make_async_copy(held.at[rows], out.at[rows], sems.at[piece]))
        copies[-1].start()
    for copy in copies:
        copy.wait()


def hop(value, second):
    energies, slabs = lax.axis_size("energy"), lax.axis_size("slab")
    bits = [2 - slab % 2 for slab in range(slabs)]
    if second:
        bits = [GROUP - 1 - bit for bit in bits]
    pairs = [
        (e * slabs + slab, (e ^ bit) * slabs + slab)
        for e in range(energies)
        for slab, bit in enumerate(bits)
    ]
    return lax.ppermute(value, ("energy", "slab"), pairs)


def across_groups(value, partner):
    groups = lax.axis_size("energy") // GROUP
    pairs = [(group, partner(group)) for group in range(groups)]
    return lax.ppermute(
        value,
        "energy",
        [(GROUP * a + i, GROUP * b + i) for a, b in pairs if 0 <= b < groups for i in range(GROUP)],
    )


def first_pair(group):
    return group ^ 1


def second_pair(group):
    return ((group + 1) ^ 1) - 1


def body(green_local, coupling, phonon_coupling, offsets, bose_factors):
    g = green_local[0]
    m = g.shape[0]
    groups = lax.axis_size("energy") // GROUP
    half = jax.ShapeDtypeStruct((m, m), jnp.bfloat16)
    taller = jax.ShapeDtypeStruct((m + 16, m), jnp.bfloat16)
    wide = jax.ShapeDtypeStruct((m, m), jnp.float32)
    line = jax.ShapeDtypeStruct((1, m), jnp.float32)

    def bank(blocks):
        return pltpu.VMEM((blocks, m, m), jnp.bfloat16)

    def totals(blocks):
        return pltpu.VMEM((blocks, m, m), jnp.float32)

    real, imag, dos = greens_halves(g, coupling)
    places = jax.ShapeDtypeStruct((8, LANES), jnp.int32)
    factors = jax.ShapeDtypeStruct((8, LANES), jnp.float32)
    table = call(mode_table, [places, factors], [offsets, bose_factors])
    modes = [phonon_coupling, *table]
    first_imag = across_groups(imag, first_pair)
    second_imag = across_groups(imag, second_pair)
    near = hop(real, False)
    reals = [real, near, hop(real, True), hop(near, True)]

    first_imag, reals[1], *table = lax.optimization_barrier((first_imag, reals[1], *table))
    modes = [phonon_coupling, *table]

    group_sum, dos_first = call(
        functools.partial(column_sums, lax.axis_size("energy")), [line, line], [first_imag, dos]
    )
    received = [dos_first]
    step = 2
    while step < groups:
        if step > 2:
            (group_sum,) = call(add_lines, [line], [group_sum, received[-1]])
        received.append(across_groups(group_sum, lambda a, step=step: a ^ step))
        step *= 2

    heights = (m + EXTRA, m + EXTRA + EXTRA_B, m + EXTRA)
    taller = [jax.ShapeDtypeStruct((h, m), jnp.bfloat16) for h in heights]
    second_imag, reals[2] = lax.optimization_barrier((second_imag, reals[2]))
    sums = call(
        to_seats,
        taller,
        [imag, first_imag, second_imag, *modes],
        [bank(3), bank(2)],
    )
    (imag_total,) = call(column_terms, [wide], [first_imag, second_imag, *modes])
    received[-1], reals[3], *sums = lax.optimization_barrier((received[-1], reals[3], *sums))
    (before,) = call(sums_before, [line], received)
    sums = call(with_lines, taller, [dos, before, *sums], aliases={2: 0, 3: 1, 4: 2})
    direct_term = hop(sums[1], False)
    (merged,) = call(merge, taller[2:], [hop(sums[0], False), sums[2]])
    seat_terms = [direct_term, hop(merged, True)]

    reals[0], _ = lax.optimization_barrier((reals[0], sums[0]))
    for_groups = jax.ShapeDtypeStruct((m + EXTRA_C, m), jnp.bfloat16)
    first_out, second_out = call(
        to_groups, [for_groups] * 2, [*reals, *modes], [bank(GROUP - 1), totals(2)]
    )
    first_term = across_groups(first_out, first_pair)
    second_term = across_groups(second_out, second_pair)
    (real_total,) = call(group_terms, [wide], [*reals[1:], *modes], [bank(GROUP - 1)])

    pieces = 4 if m % 64 == 0 else 1
    sigma, cumulative = call(
        last_sum,
        [jax.ShapeDtypeStruct(g.shape, jnp.bfloat16), line],
        [real_total, imag_total, first_term, second_term, before, dos, *seat_terms],
        [
            pltpu.VMEM(g.shape, jnp.bfloat16),
            pltpu.VMEM((1, m), jnp.float32),
            pltpu.SemaphoreType.DMA((pieces,)),
            pltpu.SemaphoreType.DMA,
        ],
        outside=(0, 1),
    )
    return sigma[None], cumulative


def solution(mesh):
    in_specs = (P("energy", "slab", None), P("slab", None), P(), P(), P())
    out_specs = (P("energy", "slab", None), P("energy", "slab"))
    return jax.shard_map(body, mesh=mesh, in_specs=in_specs, out_specs=out_specs, check_vma=False)
```

```python
import functools

import jax
import jax.numpy as jnp
from jax import lax
from jax.experimental import pallas as pl
from jax.experimental.pallas import tpu as pltpu
from jax.sharding import PartitionSpec as P

OMAX = 4
GROUP = OMAX
EXTRA = 16
EXTRA_C = 16
EXTRA_B = 16
LANES = 128
VMEM_LIMIT = 16 * 1024 * 1024

WHOLE = pl.BlockSpec(memory_space=pltpu.VMEM)
OUTSIDE = pl.BlockSpec(memory_space=pl.ANY)
SCALARS = pl.BlockSpec(memory_space=pltpu.SMEM)


def nn(a, b):
    return lax.dot_general(a, b, (((1,), (0,)), ((), ())), preferred_element_type=jnp.float32)


def nt(a, b):
    return lax.dot_general(a, b, (((1,), (1,)), ((), ())), preferred_element_type=jnp.float32)


def tn(a, b):
    return lax.dot_general(a, b, (((0,), (0,)), ((), ())), preferred_element_type=jnp.float32)


def bf(value):
    return value.astype(jnp.bfloat16)


def f32(value):
    return value.astype(jnp.float32)


def call(kernel, outs, ins, scratch=(), flops=0, aliases=None, outside=()):
    return pl.pallas_call(
        kernel,
        out_shape=outs,
        in_specs=[SCALARS if i.ndim == 1 else WHOLE for i in ins],
        out_specs=[OUTSIDE if o in outside else WHOLE for o in range(len(outs))],
        scratch_shapes=scratch,
        input_output_aliases=aliases or {},
        compiler_params=pltpu.CompilerParams(vmem_limit_bytes=VMEM_LIMIT),
        cost_estimate=pl.CostEstimate(flops=flops, bytes_accessed=0, transcendentals=0),
    )(*ins)


def upper_term(link, block):
    m = link.shape[0]
    left = bf(nn(link, block))
    return bf(nt(left[:, :m], link)), bf(nt(left[:, m:], link))


def lower_term(link, block):
    m = link.shape[0]
    left = bf(tn(link, block))
    return bf(nn(left[:, :m], link)), bf(nn(left[:, m:], link))


def rotated(block):
    m = block.shape[0]
    return jnp.concatenate([-block[:, m:], block[:, :m]], axis=1)


def complex_product(first, second):
    return nn(first, jnp.concatenate([second, rotated(second)], axis=0))


def holes_at(energy, energies, shape):
    position = jnp.full(shape, f32(energy), jnp.float32)
    return 1.0 / (1.0 + jnp.exp(-((position + 0.5 - energies / 2) * 4.0 / energies)))


def hole_line(energies, out):
    out[...] = holes_at(lax.axis_index("energy"), energies, out.shape)


def mode_table(offsets_ref, bose_ref, places_out, factors_out):
    assert offsets_ref.shape == (3,)
    far = jnp.where(offsets_ref[1] == GROUP, 1, jnp.where(offsets_ref[2] == GROUP, 2, 0))
    one, two = jnp.where(far == 0, 1, 0), jnp.where(far == 2, 1, 2)
    odd = jnp.where(lax.rem(offsets_ref[one], 2) == 1, one, two)
    for row, mode in enumerate((far, odd, one + two - odd)):
        places_out[row : row + 1] = jnp.full((1, LANES), mode, jnp.int32)
        places_out[row + 3 : row + 4] = jnp.full((1, LANES), offsets_ref[mode], jnp.int32)
        factors_out[row : row + 1] = jnp.full((1, LANES), bose_ref[mode], jnp.float32)


def modes_of(phonon_ref, places_ref, factors_ref):
    return [(places_ref[row, 0], places_ref[row + 3, 0], factors_ref[row, 0]) for row in range(3)]


def diagonal_of(block_ref):
    m = block_ref.shape[0]
    tile = 128 if m % 128 == 0 else m
    rows = lax.broadcasted_iota(jnp.int32, (tile, tile), 0)
    columns = lax.broadcasted_iota(jnp.int32, (tile, tile), 1)
    parts = []
    for start in range(0, m, tile):
        block = f32(block_ref[start : start + tile, start : start + tile])
        parts.append(jnp.sum(jnp.where(rows == columns, block, 0.0), axis=0, keepdims=True))
    return jnp.concatenate(parts, axis=1)


def finish(g, dressed, holes_ref, real_ref, imag_ref, dos_ref):
    m = g.shape[0]
    greens = bf(f32(g) + complex_product(dressed, g) / m)
    real_ref[...] = greens[:, :m]
    imag_ref[...] = greens[:, m:]
    dos_ref[...] = -holes_ref[...] * diagonal_of(imag_ref)


def greens_of_first(g_ref, other_ref, own_ref, holes_ref, *rest):
    *outs, couple = rest

    @pl.when(lax.axis_index("slab") == 0)
    def _():
        m = own_ref.shape[0]
        couple[:, :m], couple[:, m:] = upper_term(own_ref[...], other_ref[...])
        g = g_ref[...]
        finish(g, bf(complex_product(g, couple[...])), holes_ref, *outs)


def greens_of_second(g_ref, other_ref, below_ref, holes_ref, *rest):
    kept, (*outs, couple) = rest[:3], rest[3:]

    @pl.when(lax.axis_index("slab") == 0)
    def _():
        for out, value in zip(outs, kept):
            out[...] = value[...]

    @pl.when(lax.axis_index("slab") != 0)
    def _():
        m = below_ref.shape[0]
        couple[:, :m], couple[:, m:] = lower_term(below_ref[...], other_ref[...])
        g = g_ref[...]
        finish(g, bf(complex_product(g, couple[...])), holes_ref, *outs)


def greens_of_chain(g_ref, above_ref, lower_ref, own_ref, below_ref, holes_ref, *outs):
    up_real, up_imag = upper_term(own_ref[...], above_ref[...])
    low_real, low_imag = lower_term(below_ref[...], lower_ref[...])
    real = bf(f32(up_real) + f32(low_real))
    imag = bf(f32(up_imag) + f32(low_imag))
    g = g_ref[...]
    couple = jnp.concatenate([real, imag], axis=1)
    finish(g, bf(complex_product(g, couple)), holes_ref, *outs)


def greens_halves(g, coupling):
    m = g.shape[0]
    slabs = lax.axis_size("slab")
    half = jax.ShapeDtypeStruct((m, m), jnp.bfloat16)
    line = jax.ShapeDtypeStruct((1, m), jnp.float32)
    outs = [half, half, line]
    up = [(s, s + 1) for s in range(slabs - 1)]
    down = [(s + 1, s) for s in range(slabs - 1)]
    below = lax.ppermute(coupling, "slab", up)
    energies = lax.axis_size("energy")
    (holes,) = call(functools.partial(hole_line, energies), [line], [], flops=24 * m**3)
    if slabs == 2:
        other = lax.ppermute(g, "slab", up + down)
        couple = [pltpu.VMEM(g.shape, jnp.bfloat16)]
        first = call(greens_of_first, outs, [g, other, coupling, holes], couple)
        ins = [g, other, below, holes, *first]
        return call(greens_of_second, outs, ins, couple, aliases={4: 0, 5: 1, 6: 2})
    above = lax.ppermute(g, "slab", down)
    lower = lax.ppermute(g, "slab", up)
    return call(greens_of_chain, outs, [g, above, lower, coupling, below, holes])


def place():
    energy = lax.axis_index("energy")
    group = lax.div(energy, jnp.int32(GROUP))
    seat = lax.rem(energy, jnp.int32(GROUP))
    return energy, group, seat


def hops():
    bit = 1 + lax.rem(lax.axis_index("slab"), 2)
    return bit, (GROUP - 1) - bit


def first_side(group):
    return 1 - 2 * lax.rem(group, jnp.int32(2))


def product(matrix, block, scale=None):
    left = nn(matrix, block)
    return nt(bf(left if scale is None else scale * left), matrix)


def mixed(first, first_weight, second, second_weight):
    return bf(first_weight * f32(first) + second_weight * f32(second))


def split_rows(line):
    high = bf(line)
    rest = line - f32(high)
    middle = bf(rest)
    low = bf(rest - f32(middle))
    rows = [f32(high), f32(middle), f32(low), jnp.zeros((EXTRA - 3, line.shape[1]), jnp.float32)]
    return bf(jnp.concatenate(rows, axis=0))


def to_seats(own_ref, first_ref, second_ref, phonon_ref, places_ref, factors_ref, *rest):
    across, direct, merged, bank, sums = rest
    m = own_ref.shape[0]
    _, group, seat = place()
    side = first_side(group)
    bank[0] = own_ref[...]
    bank[1] = first_ref[...]
    bank[2] = second_ref[...]
    _, odd, left = modes_of(phonon_ref, places_ref, factors_ref)

    def towards(j):
        apart = jnp.bitwise_xor(seat, j) - seat
        upward = apart > 0
        beside = jnp.where(upward == (side > 0), 1, 2)
        return jnp.abs(apart), upward, beside

    def odd_seats(mode):
        index, shift, factor = mode
        blocks, weights = [], []
        for j in (1, 3):
            size, upward, beside = towards(j)
            own = shift == size
            blocks.append(bank[jnp.where(own, 0, beside)])
            weights.append(jnp.where(own == upward, factor + 1.0, factor))
        matrix = phonon_ref[index]
        wide = nn(matrix, jnp.concatenate(blocks, axis=1))
        parts = [bf(w * wide[:, i * m : (i + 1) * m]) for i, w in enumerate(weights)]
        return nt(jnp.concatenate(parts, axis=0), matrix)

    def put(wide):
        sums[0] = bf(wide[:m])
        across[:m] = bf(wide[m:])

    index, shift, factor = left

    @pl.when(lax.rem(shift, 2) == 0)
    def _():
        wide = odd_seats(odd)
        _, upward, beside = towards(2)
        own_weight = jnp.where(upward, factor + 1.0, factor)
        beside_weight = jnp.where(upward, factor, factor + 1.0)
        block = mixed(bank[0], own_weight, bank[beside], beside_weight)
        sums[1] = bf(product(phonon_ref[index], block))
        put(wide)

    @pl.when(lax.rem(shift, 2) == 1)
    def _():
        put(odd_seats(odd) + odd_seats(left))
        sums[1] = jnp.zeros((m, m), jnp.bfloat16)

    first, second = hops()
    direct[:m] = sums[first - 1]
    merged[:m] = sums[second - 1]


def with_lines(dos_ref, before_ref, *refs):
    m = dos_ref.shape[1]
    _, _, seat = place()
    first, second = hops()
    for kept, out, j in zip(refs[:3], refs[3:], (GROUP - 1, first, second)):
        out[:m] = kept[:m]
        counts = jnp.bitwise_xor(seat, j) > seat
        out[m : m + EXTRA] = split_rows(
            before_ref[...] + jnp.where(counts, dos_ref[...], 0.0)
        )
        if out.shape[0] > m + EXTRA:
            out[m + EXTRA :] = jnp.zeros((out.shape[0] - m - EXTRA, m), jnp.bfloat16)


def merge(received_ref, merged_ref, out):
    m = received_ref.shape[1]
    out[:m] = bf(f32(merged_ref[:m]) + f32(received_ref[:m]))
    lines = f32(merged_ref[m : m + EXTRA]) + f32(received_ref[m : m + EXTRA])
    out[m : m + EXTRA] = split_rows(jnp.sum(lines, axis=0, keepdims=True))


def to_groups(*refs):
    parts, (phonon_ref, places_ref, factors_ref) = refs[:GROUP], refs[GROUP : GROUP + 3]
    first_out, second_out, bank, total = refs[GROUP + 3 :]
    _, group, seat = place()
    upward = seat < GROUP // 2
    first, second = hops()
    for j, part in zip((first, second, GROUP - 1), parts[1:]):
        bank[j - 1] = part[...]
    modes = modes_of(phonon_ref, places_ref, factors_ref)

    def gives(shift, factor, up):
        source = seat + jnp.where(up, GROUP - shift, shift - GROUP)
        inside = jnp.logical_and(source >= 0, source < GROUP)
        place_of = jnp.where(inside, jnp.bitwise_xor(seat, source) - 1, 0)
        return inside, place_of, jnp.where(up, factor + 1.0, factor)

    most = less = None
    for index, shift, factor in modes:
        inside, place_of, weight = gives(shift, factor, upward)
        block = parts[0][...] if most is None else bank[place_of]
        whole = product(phonon_ref[index], block)
        term = jnp.where(inside, weight, 0.0) * whole
        if most is None:
            most, less = term, gives(shift, factor, jnp.logical_not(upward))[2] * whole
        else:
            most = most + term
    total[0] = most
    total[1] = less
    for index, shift, factor in modes[1:]:
        inside, place_of, weight = gives(shift, factor, jnp.logical_not(upward))

        @pl.when(inside)
        def _(index=index, place_of=place_of, weight=weight):
            total[1] += product(phonon_ref[index], bank[place_of], weight)

    most_first = upward == (first_side(group) > 0)
    m = bank.shape[1]
    first_out[:m] = bf(total[jnp.where(most_first, 0, 1)])
    second_out[:m] = bf(total[jnp.where(most_first, 1, 0)])
    for out in (first_out, second_out) if first_out.shape[0] > m else ():
        out[m:] = jnp.zeros((out.shape[0] - m, m), jnp.bfloat16)


def column_terms(first_ref, second_ref, phonon_ref, places_ref, factors_ref, out):
    _, group, _ = place()
    side = first_side(group)
    (index, _, factor), _, _ = modes_of(phonon_ref, places_ref, factors_ref)
    first_weight = jnp.where(side > 0, factor, factor + 1.0)
    second_weight = jnp.where(side > 0, factor + 1.0, factor)
    block = mixed(first_ref[...], first_weight, second_ref[...], second_weight)
    out[...] = product(phonon_ref[index], block)


def group_terms(*refs):
    parts, (phonon_ref, places_ref, factors_ref, out, bank) = refs[: GROUP - 1], refs[GROUP - 1 :]
    _, _, seat = place()
    first, second = hops()
    for j, part in zip((first, second, GROUP - 1), parts):
        bank[j - 1] = part[...]
    sum_of_modes = None
    for index, shift, factor in modes_of(phonon_ref, places_ref, factors_ref)[1:]:
        below, above = seat - shift, seat + shift
        has_below, has_above = below >= 0, above < GROUP
        first = jnp.where(has_below, jnp.bitwise_xor(seat, below) - 1, 0)
        second = jnp.where(has_above, jnp.bitwise_xor(seat, above) - 1, 0)
        block = mixed(
            bank[first],
            jnp.where(has_below, factor + 1.0, 0.0),
            bank[second],
            jnp.where(has_above, factor, 0.0),
        )
        term = product(phonon_ref[index], block)
        sum_of_modes = term if sum_of_modes is None else sum_of_modes + term
    out[...] = sum_of_modes


def add_lines(a, b, out):
    out[...] = a[...] + b[...]


def column_sums(energies, first_ref, dos_ref, pair_out, dos_first_out):
    energy, group, _ = place()
    terms = -holes_at(energy + GROUP * first_side(group), energies, dos_ref.shape)
    terms = terms * diagonal_of(first_ref)
    dos_first_out[...] = terms
    pair_out[...] = terms + dos_ref[...]


def sums_before(*refs):
    *received, out = refs
    _, group, _ = place()
    line = jnp.zeros(out.shape, jnp.float32)
    for power, part in enumerate(received):
        line = line + jnp.where(jnp.bitwise_and(group, 1 << power) > 0, part[...], 0.0)
    out[...] = line


def last_sum(*refs):
    real_total, imag_total, first, second, before, dos = refs[:6]
    *seats, out, cumulative, held, line, sems, line_sem = refs[6:]
    m = real_total.shape[0]
    density = before[...] + dos[...]
    for part in seats:
        density = density + jnp.sum(f32(part[m : m + EXTRA]), axis=0, keepdims=True)
    line[...] = density
    copies = [pltpu.make_async_copy(line, cumulative, line_sem)]
    copies[0].start()
    pieces = sems.shape[0]
    for piece in range(pieces):
        rows = pl.ds(piece * (m // pieces), m // pieces)
        held[rows, :m] = bf(real_total[rows] + f32(first[rows]) + f32(second[rows]))
        imag = imag_total[rows]
        for part in seats:
            imag = imag + f32(part[rows])
        held[rows, m:] = bf(imag)
        copies.append(pltpu.make_async_copy(held.at[rows], out.at[rows], sems.at[piece]))
        copies[-1].start()
    for copy in copies:
        copy.wait()


def hop(value, second):
    energies, slabs = lax.axis_size("energy"), lax.axis_size("slab")
    bits = [1 + slab % 2 for slab in range(slabs)]
    if second:
        bits = [GROUP - 1 - bit for bit in bits]
    pairs = [
        (e * slabs + slab, (e ^ bit) * slabs + slab)
        for e in range(energies)
        for slab, bit in enumerate(bits)
    ]
    return lax.ppermute(value, ("energy", "slab"), pairs)


def across_groups(value, partner):
    groups = lax.axis_size("energy") // GROUP
    pairs = [(group, partner(group)) for group in range(groups)]
    return lax.ppermute(
        value,
        "energy",
        [(GROUP * a + i, GROUP * b + i) for a, b in pairs if 0 <= b < groups for i in range(GROUP)],
    )


def first_pair(group):
    return group ^ 1


def second_pair(group):
    return ((group + 1) ^ 1) - 1


def body(green_local, coupling, phonon_coupling, offsets, bose_factors):
    g = green_local[0]
    m = g.shape[0]
    groups = lax.axis_size("energy") // GROUP
    half = jax.ShapeDtypeStruct((m, m), jnp.bfloat16)
    taller = jax.ShapeDtypeStruct((m + 16, m), jnp.bfloat16)
    wide = jax.ShapeDtypeStruct((m, m), jnp.float32)
    line = jax.ShapeDtypeStruct((1, m), jnp.float32)

    def bank(blocks):
        return pltpu.VMEM((blocks, m, m), jnp.bfloat16)

    def totals(blocks):
        return pltpu.VMEM((blocks, m, m), jnp.float32)

    real, imag, dos = greens_halves(g, coupling)
    places = jax.ShapeDtypeStruct((8, LANES), jnp.int32)
    factors = jax.ShapeDtypeStruct((8, LANES), jnp.float32)
    table = call(mode_table, [places, factors], [offsets, bose_factors])
    modes = [phonon_coupling, *table]
    first_imag = across_groups(imag, first_pair)
    second_imag = across_groups(imag, second_pair)
    near = hop(real, False)
    reals = [real, near, hop(real, True), hop(near, True)]

    first_imag, reals[1], *table = lax.optimization_barrier((first_imag, reals[1], *table))
    modes = [phonon_coupling, *table]

    group_sum, dos_first = call(
        functools.partial(column_sums, lax.axis_size("energy")), [line, line], [first_imag, dos]
    )
    received = [dos_first]
    step = 2
    while step < groups:
        if step > 2:
            (group_sum,) = call(add_lines, [line], [group_sum, received[-1]])
        received.append(across_groups(group_sum, lambda a, step=step: a ^ step))
        step *= 2

    heights = (m + EXTRA, m + EXTRA + EXTRA_B, m + EXTRA)
    taller = [jax.ShapeDtypeStruct((h, m), jnp.bfloat16) for h in heights]
    second_imag, reals[2] = lax.optimization_barrier((second_imag, reals[2]))
    sums = call(
        to_seats,
        taller,
        [imag, first_imag, second_imag, *modes],
        [bank(3), bank(2)],
    )
    (imag_total,) = call(column_terms, [wide], [first_imag, second_imag, *modes])
    received[-1], reals[3], *sums = lax.optimization_barrier((received[-1], reals[3], *sums))
    (before,) = call(sums_before, [line], received)
    sums = call(with_lines, taller, [dos, before, *sums], aliases={2: 0, 3: 1, 4: 2})
    direct_term = hop(sums[1], False)
    (merged,) = call(merge, taller[2:], [hop(sums[0], False), sums[2]])
    seat_terms = [direct_term, hop(merged, True)]

    reals[0], _ = lax.optimization_barrier((reals[0], sums[0]))
    for_groups = jax.ShapeDtypeStruct((m + EXTRA_C, m), jnp.bfloat16)
    first_out, second_out = call(
        to_groups, [for_groups] * 2, [*reals, *modes], [bank(GROUP - 1), totals(2)]
    )
    first_term = across_groups(first_out, first_pair)
    second_term = across_groups(second_out, second_pair)
    (real_total,) = call(group_terms, [wide], [*reals[1:], *modes], [bank(GROUP - 1)])

    pieces = 2 if m % 32 == 0 else 1
    sigma, cumulative = call(
        last_sum,
        [jax.ShapeDtypeStruct(g.shape, jnp.bfloat16), line],
        [real_total, imag_total, first_term, second_term, before, dos, *seat_terms],
        [
            pltpu.VMEM(g.shape, jnp.bfloat16),
            pltpu.VMEM((1, m), jnp.float32),
            pltpu.SemaphoreType.DMA((pieces,)),
            pltpu.SemaphoreType.DMA,
        ],
        outside=(0, 1),
    )
    return sigma[None], cumulative


def solution(mesh):
    in_specs = (P("energy", "slab", None), P("slab", None), P(), P(), P())
    out_specs = (P("energy", "slab", None), P("energy", "slab"))
    return jax.shard_map(body, mesh=mesh, in_specs=in_specs, out_specs=out_specs, check_vma=False)
```

```python
import functools

import jax
import jax.numpy as jnp
from jax import lax
from jax.experimental import pallas as pl
from jax.experimental.pallas import tpu as pltpu
from jax.sharding import PartitionSpec as P

OMAX = 4
GROUP = OMAX
EXTRA = 16
EXTRA_C = 16
EXTRA_B = 16
LANES = 128
VMEM_LIMIT = 16 * 1024 * 1024

WHOLE = pl.BlockSpec(memory_space=pltpu.VMEM)
OUTSIDE = pl.BlockSpec(memory_space=pl.ANY)
SCALARS = pl.BlockSpec(memory_space=pltpu.SMEM)


def nn(a, b):
    return lax.dot_general(a, b, (((1,), (0,)), ((), ())), preferred_element_type=jnp.float32)


def nt(a, b):
    return lax.dot_general(a, b, (((1,), (1,)), ((), ())), preferred_element_type=jnp.float32)


def tn(a, b):
    return lax.dot_general(a, b, (((0,), (0,)), ((), ())), preferred_element_type=jnp.float32)


def bf(value):
    return value.astype(jnp.bfloat16)


def f32(value):
    return value.astype(jnp.float32)


def call(kernel, outs, ins, scratch=(), flops=0, aliases=None, outside=()):
    return pl.pallas_call(
        kernel,
        out_shape=outs,
        in_specs=[SCALARS if i.ndim == 1 else WHOLE for i in ins],
        out_specs=[OUTSIDE if o in outside else WHOLE for o in range(len(outs))],
        scratch_shapes=scratch,
        input_output_aliases=aliases or {},
        compiler_params=pltpu.CompilerParams(vmem_limit_bytes=VMEM_LIMIT),
        cost_estimate=pl.CostEstimate(flops=flops, bytes_accessed=0, transcendentals=0),
    )(*ins)


def upper_term(link, block):
    m = link.shape[0]
    left = bf(nn(link, block))
    return bf(nt(left[:, :m], link)), bf(nt(left[:, m:], link))


def lower_term(link, block):
    m = link.shape[0]
    left = bf(tn(link, block))
    return bf(nn(left[:, :m], link)), bf(nn(left[:, m:], link))


def rotated(block):
    m = block.shape[0]
    return jnp.concatenate([-block[:, m:], block[:, :m]], axis=1)


def complex_product(first, second):
    return nn(first, jnp.concatenate([second, rotated(second)], axis=0))


def holes_at(energy, energies, shape):
    position = jnp.full(shape, f32(energy), jnp.float32)
    return 1.0 / (1.0 + jnp.exp(-((position + 0.5 - energies / 2) * 4.0 / energies)))


def hole_line(energies, out):
    out[...] = holes_at(lax.axis_index("energy"), energies, out.shape)


def mode_table(offsets_ref, bose_ref, places_out, factors_out):
    assert offsets_ref.shape == (3,)
    far = jnp.where(offsets_ref[1] == GROUP, 1, jnp.where(offsets_ref[2] == GROUP, 2, 0))
    one, two = jnp.where(far == 0, 1, 0), jnp.where(far == 2, 1, 2)
    odd = jnp.where(lax.rem(offsets_ref[one], 2) == 1, one, two)
    for row, mode in enumerate((far, odd, one + two - odd)):
        places_out[row : row + 1] = jnp.full((1, LANES), mode, jnp.int32)
        places_out[row + 3 : row + 4] = jnp.full((1, LANES), offsets_ref[mode], jnp.int32)
        factors_out[row : row + 1] = jnp.full((1, LANES), bose_ref[mode], jnp.float32)


def modes_of(phonon_ref, places_ref, factors_ref):
    return [(places_ref[row, 0], places_ref[row + 3, 0], factors_ref[row, 0]) for row in range(3)]


def diagonal_of(block_ref):
    m = block_ref.shape[0]
    tile = 128 if m % 128 == 0 else m
    rows = lax.broadcasted_iota(jnp.int32, (tile, tile), 0)
    columns = lax.broadcasted_iota(jnp.int32, (tile, tile), 1)
    parts = []
    for start in range(0, m, tile):
        block = f32(block_ref[start : start + tile, start : start + tile])
        parts.append(jnp.sum(jnp.where(rows == columns, block, 0.0), axis=0, keepdims=True))
    return jnp.concatenate(parts, axis=1)


def finish(g, dressed, holes_ref, real_ref, imag_ref, dos_ref):
    m = g.shape[0]
    greens = bf(f32(g) + complex_product(dressed, g) / m)
    real_ref[...] = greens[:, :m]
    imag_ref[...] = greens[:, m:]
    dos_ref[...] = -holes_ref[...] * diagonal_of(imag_ref)


def greens_of_first(g_ref, other_ref, own_ref, holes_ref, *rest):
    *outs, couple = rest

    @pl.when(lax.axis_index("slab") == 0)
    def _():
        m = own_ref.shape[0]
        couple[:, :m], couple[:, m:] = upper_term(own_ref[...], other_ref[...])
        g = g_ref[...]
        finish(g, bf(complex_product(g, couple[...])), holes_ref, *outs)


def greens_of_second(g_ref, other_ref, below_ref, holes_ref, *rest):
    kept, (*outs, couple) = rest[:3], rest[3:]

    @pl.when(lax.axis_index("slab") == 0)
    def _():
        for out, value in zip(outs, kept):
            out[...] = value[...]

    @pl.when(lax.axis_index("slab") != 0)
    def _():
        m = below_ref.shape[0]
        couple[:, :m], couple[:, m:] = lower_term(below_ref[...], other_ref[...])
        g = g_ref[...]
        finish(g, bf(complex_product(g, couple[...])), holes_ref, *outs)


def greens_of_chain(g_ref, above_ref, lower_ref, own_ref, below_ref, holes_ref, *outs):
    up_real, up_imag = upper_term(own_ref[...], above_ref[...])
    low_real, low_imag = lower_term(below_ref[...], lower_ref[...])
    real = bf(f32(up_real) + f32(low_real))
    imag = bf(f32(up_imag) + f32(low_imag))
    g = g_ref[...]
    couple = jnp.concatenate([real, imag], axis=1)
    finish(g, bf(complex_product(g, couple)), holes_ref, *outs)


def greens_halves(g, coupling):
    m = g.shape[0]
    slabs = lax.axis_size("slab")
    half = jax.ShapeDtypeStruct((m, m), jnp.bfloat16)
    line = jax.ShapeDtypeStruct((1, m), jnp.float32)
    outs = [half, half, line]
    up = [(s, s + 1) for s in range(slabs - 1)]
    down = [(s + 1, s) for s in range(slabs - 1)]
    below = lax.ppermute(coupling, "slab", up)
    energies = lax.axis_size("energy")
    (holes,) = call(functools.partial(hole_line, energies), [line], [], flops=24 * m**3)
    if slabs == 2:
        other = lax.ppermute(g, "slab", up + down)
        couple = [pltpu.VMEM(g.shape, jnp.bfloat16)]
        first = call(greens_of_first, outs, [g, other, coupling, holes], couple)
        ins = [g, other, below, holes, *first]
        return call(greens_of_second, outs, ins, couple, aliases={4: 0, 5: 1, 6: 2})
    above = lax.ppermute(g, "slab", down)
    lower = lax.ppermute(g, "slab", up)
    return call(greens_of_chain, outs, [g, above, lower, coupling, below, holes])


def place():
    energy = lax.axis_index("energy")
    group = lax.div(energy, jnp.int32(GROUP))
    seat = lax.rem(energy, jnp.int32(GROUP))
    return energy, group, seat


def hops():
    bit = 2 - lax.rem(lax.axis_index("slab"), 2)
    return bit, (GROUP - 1) - bit


def first_side(group):
    return 1 - 2 * lax.rem(group, jnp.int32(2))


def product(matrix, block, scale=None):
    left = nn(matrix, block)
    return nt(bf(left if scale is None else scale * left), matrix)


def mixed(first, first_weight, second, second_weight):
    return bf(first_weight * f32(first) + second_weight * f32(second))


def split_rows(line):
    high = bf(line)
    rest = line - f32(high)
    middle = bf(rest)
    low = bf(rest - f32(middle))
    rows = [f32(high), f32(middle), f32(low), jnp.zeros((EXTRA - 3, line.shape[1]), jnp.float32)]
    return bf(jnp.concatenate(rows, axis=0))


def to_seats(own_ref, first_ref, second_ref, phonon_ref, places_ref, factors_ref, *rest):
    across, direct, merged, bank, sums = rest
    m = own_ref.shape[0]
    _, group, seat = place()
    side = first_side(group)
    bank[0] = own_ref[...]
    bank[1] = first_ref[...]
    bank[2] = second_ref[...]
    _, odd, left = modes_of(phonon_ref, places_ref, factors_ref)

    def towards(j):
        apart = jnp.bitwise_xor(seat, j) - seat
        upward = apart > 0
        beside = jnp.where(upward == (side > 0), 1, 2)
        return jnp.abs(apart), upward, beside

    def odd_seats(mode):
        index, shift, factor = mode
        blocks, weights = [], []
        for j in (1, 3):
            size, upward, beside = towards(j)
            own = shift == size
            blocks.append(bank[jnp.where(own, 0, beside)])
            weights.append(jnp.where(own == upward, factor + 1.0, factor))
        matrix = phonon_ref[index]
        wide = nn(matrix, jnp.concatenate(blocks, axis=1))
        parts = [bf(w * wide[:, i * m : (i + 1) * m]) for i, w in enumerate(weights)]
        return nt(jnp.concatenate(parts, axis=0), matrix)

    def put(wide):
        sums[0] = bf(wide[:m])
        across[:m] = bf(wide[m:])

    index, shift, factor = left

    @pl.when(lax.rem(shift, 2) == 0)
    def _():
        wide = odd_seats(odd)
        _, upward, beside = towards(2)
        own_weight = jnp.where(upward, factor + 1.0, factor)
        beside_weight = jnp.where(upward, factor, factor + 1.0)
        block = mixed(bank[0], own_weight, bank[beside], beside_weight)
        sums[1] = bf(product(phonon_ref[index], block))
        put(wide)

    @pl.when(lax.rem(shift, 2) == 1)
    def _():
        put(odd_seats(odd) + odd_seats(left))
        sums[1] = jnp.zeros((m, m), jnp.bfloat16)

    first, second = hops()
    direct[:m] = sums[first - 1]
    merged[:m] = sums[second - 1]


def with_lines(dos_ref, before_ref, *refs):
    m = dos_ref.shape[1]
    _, _, seat = place()
    first, second = hops()
    for kept, out, j in zip(refs[:3], refs[3:], (GROUP - 1, first, second)):
        out[:m] = kept[:m]
        counts = jnp.bitwise_xor(seat, j) > seat
        out[m : m + EXTRA] = split_rows(
            before_ref[...] + jnp.where(counts, dos_ref[...], 0.0)
        )
        if out.shape[0] > m + EXTRA:
            out[m + EXTRA :] = jnp.zeros((out.shape[0] - m - EXTRA, m), jnp.bfloat16)


def merge(received_ref, merged_ref, out):
    m = received_ref.shape[1]
    out[:m] = bf(f32(merged_ref[:m]) + f32(received_ref[:m]))
    lines = f32(merged_ref[m : m + EXTRA]) + f32(received_ref[m : m + EXTRA])
    out[m : m + EXTRA] = split_rows(jnp.sum(lines, axis=0, keepdims=True))


def to_groups(*refs):
    parts, (phonon_ref, places_ref, factors_ref) = refs[:GROUP], refs[GROUP : GROUP + 3]
    first_out, second_out, bank, total = refs[GROUP + 3 :]
    _, group, seat = place()
    upward = seat < GROUP // 2
    first, second = hops()
    for j, part in zip((first, second, GROUP - 1), parts[1:]):
        bank[j - 1] = part[...]
    modes = modes_of(phonon_ref, places_ref, factors_ref)

    def gives(shift, factor, up):
        source = seat + jnp.where(up, GROUP - shift, shift - GROUP)
        inside = jnp.logical_and(source >= 0, source < GROUP)
        place_of = jnp.where(inside, jnp.bitwise_xor(seat, source) - 1, 0)
        return inside, place_of, jnp.where(up, factor + 1.0, factor)

    most = less = None
    for index, shift, factor in modes:
        inside, place_of, weight = gives(shift, factor, upward)
        block = parts[0][...] if most is None else bank[place_of]
        whole = product(phonon_ref[index], block)
        term = jnp.where(inside, weight, 0.0) * whole
        if most is None:
            most, less = term, gives(shift, factor, jnp.logical_not(upward))[2] * whole
        else:
            most = most + term
    total[0] = most
    total[1] = less
    for index, shift, factor in modes[1:]:
        inside, place_of, weight = gives(shift, factor, jnp.logical_not(upward))

        @pl.when(inside)
        def _(index=index, place_of=place_of, weight=weight):
            total[1] += product(phonon_ref[index], bank[place_of], weight)

    most_first = upward == (first_side(group) > 0)
    m = bank.shape[1]
    first_out[:m] = bf(total[jnp.where(most_first, 0, 1)])
    second_out[:m] = bf(total[jnp.where(most_first, 1, 0)])
    for out in (first_out, second_out) if first_out.shape[0] > m else ():
        out[m:] = jnp.zeros((out.shape[0] - m, m), jnp.bfloat16)


def column_terms(first_ref, second_ref, phonon_ref, places_ref, factors_ref, out):
    _, group, _ = place()
    side = first_side(group)
    (index, _, factor), _, _ = modes_of(phonon_ref, places_ref, factors_ref)
    first_weight = jnp.where(side > 0, factor, factor + 1.0)
    second_weight = jnp.where(side > 0, factor + 1.0, factor)
    block = mixed(first_ref[...], first_weight, second_ref[...], second_weight)
    out[...] = product(phonon_ref[index], block)


def group_terms(*refs):
    parts, (phonon_ref, places_ref, factors_ref, out, bank) = refs[: GROUP - 1], refs[GROUP - 1 :]
    _, _, seat = place()
    first, second = hops()
    for j, part in zip((first, second, GROUP - 1), parts):
        bank[j - 1] = part[...]
    sum_of_modes = None
    for index, shift, factor in modes_of(phonon_ref, places_ref, factors_ref)[1:]:
        below, above = seat - shift, seat + shift
        has_below, has_above = below >= 0, above < GROUP
        first = jnp.where(has_below, jnp.bitwise_xor(seat, below) - 1, 0)
        second = jnp.where(has_above, jnp.bitwise_xor(seat, above) - 1, 0)
        block = mixed(
            bank[first],
            jnp.where(has_below, factor + 1.0, 0.0),
            bank[second],
            jnp.where(has_above, factor, 0.0),
        )
        term = product(phonon_ref[index], block)
        sum_of_modes = term if sum_of_modes is None else sum_of_modes + term
    out[...] = sum_of_modes


def add_lines(a, b, out):
    out[...] = a[...] + b[...]


def column_sums(energies, first_ref, dos_ref, pair_out, dos_first_out):
    energy, group, _ = place()
    terms = -holes_at(energy + GROUP * first_side(group), energies, dos_ref.shape)
    terms = terms * diagonal_of(first_ref)
    dos_first_out[...] = terms
    pair_out[...] = terms + dos_ref[...]


def sums_before(*refs):
    *received, out = refs
    _, group, _ = place()
    line = jnp.zeros(out.shape, jnp.float32)
    for power, part in enumerate(received):
        line = line + jnp.where(jnp.bitwise_and(group, 1 << power) > 0, part[...], 0.0)
    out[...] = line


def last_sum(*refs):
    real_total, imag_total, first, second, before, dos = refs[:6]
    *seats, out, cumulative, held, line, sems, line_sem = refs[6:]
    m = real_total.shape[0]
    density = before[...] + dos[...]
    for part in seats:
        density = density + jnp.sum(f32(part[m : m + EXTRA]), axis=0, keepdims=True)
    line[...] = density
    copies = [pltpu.make_async_copy(line, cumulative, line_sem)]
    copies[0].start()
    pieces = sems.shape[0]
    for piece in range(pieces):
        rows = pl.ds(piece * (m // pieces), m // pieces)
        held[rows, :m] = bf(real_total[rows] + f32(first[rows]) + f32(second[rows]))
        imag = imag_total[rows]
        for part in seats:
            imag = imag + f32(part[rows])
        held[rows, m:] = bf(imag)
        copies.append(pltpu.make_async_copy(held.at[rows], out.at[rows], sems.at[piece]))
        copies[-1].start()
    for copy in copies:
        copy.wait()


def hop(value, second):
    energies, slabs = lax.axis_size("energy"), lax.axis_size("slab")
    bits = [2 - slab % 2 for slab in range(slabs)]
    if second:
        bits = [GROUP - 1 - bit for bit in bits]
    pairs = [
        (e * slabs + slab, (e ^ bit) * slabs + slab)
        for e in range(energies)
        for slab, bit in enumerate(bits)
    ]
    return lax.ppermute(value, ("energy", "slab"), pairs)


def across_groups(value, partner):
    groups = lax.axis_size("energy") // GROUP
    pairs = [(group, partner(group)) for group in range(groups)]
    return lax.ppermute(
        value,
        "energy",
        [(GROUP * a + i, GROUP * b + i) for a, b in pairs if 0 <= b < groups for i in range(GROUP)],
    )


def first_pair(group):
    return group ^ 1


def second_pair(group):
    return ((group + 1) ^ 1) - 1


def body(green_local, coupling, phonon_coupling, offsets, bose_factors):
    g = green_local[0]
    m = g.shape[0]
    groups = lax.axis_size("energy") // GROUP
    half = jax.ShapeDtypeStruct((m, m), jnp.bfloat16)
    taller = jax.ShapeDtypeStruct((m + 16, m), jnp.bfloat16)
    wide = jax.ShapeDtypeStruct((m, m), jnp.float32)
    line = jax.ShapeDtypeStruct((1, m), jnp.float32)

    def bank(blocks):
        return pltpu.VMEM((blocks, m, m), jnp.bfloat16)

    def totals(blocks):
        return pltpu.VMEM((blocks, m, m), jnp.float32)

    real, imag, dos = greens_halves(g, coupling)
    places = jax.ShapeDtypeStruct((8, LANES), jnp.int32)
    factors = jax.ShapeDtypeStruct((8, LANES), jnp.float32)
    table = call(mode_table, [places, factors], [offsets, bose_factors])
    modes = [phonon_coupling, *table]
    first_imag = across_groups(imag, first_pair)
    second_imag = across_groups(imag, second_pair)
    near = hop(real, False)
    reals = [real, near, hop(real, True), hop(near, True)]

    first_imag, reals[1], *table = lax.optimization_barrier((first_imag, reals[1], *table))
    modes = [phonon_coupling, *table]

    group_sum, dos_first = call(
        functools.partial(column_sums, lax.axis_size("energy")), [line, line], [first_imag, dos]
    )
    received = [dos_first]
    step = 2
    while step < groups:
        if step > 2:
            (group_sum,) = call(add_lines, [line], [group_sum, received[-1]])
        received.append(across_groups(group_sum, lambda a, step=step: a ^ step))
        step *= 2

    heights = (m + EXTRA, m + EXTRA + EXTRA_B, m + EXTRA)
    taller = [jax.ShapeDtypeStruct((h, m), jnp.bfloat16) for h in heights]
    second_imag, reals[2] = lax.optimization_barrier((second_imag, reals[2]))
    sums = call(
        to_seats,
        taller,
        [imag, first_imag, second_imag, *modes],
        [bank(3), bank(2)],
    )
    (imag_total,) = call(column_terms, [wide], [first_imag, second_imag, *modes])
    received[-1], reals[3], *sums = lax.optimization_barrier((received[-1], reals[3], *sums))
    (before,) = call(sums_before, [line], received)
    sums = call(with_lines, taller, [dos, before, *sums], aliases={2: 0, 3: 1, 4: 2})
    direct_term = hop(sums[1], False)
    (merged,) = call(merge, taller[2:], [hop(sums[0], False), sums[2]])
    seat_terms = [direct_term, hop(merged, True)]

    reals[0], _ = lax.optimization_barrier((reals[0], sums[0]))
    for_groups = jax.ShapeDtypeStruct((m + EXTRA_C, m), jnp.bfloat16)
    first_out, second_out = call(
        to_groups, [for_groups] * 2, [*reals, *modes], [bank(GROUP - 1), totals(2)]
    )
    first_term = across_groups(first_out, first_pair)
    second_term = across_groups(second_out, second_pair)
    (real_total,) = call(group_terms, [wide], [*reals[1:], *modes], [bank(GROUP - 1)])

    pieces = 2 if m % 32 == 0 else 1
    sigma, cumulative = call(
        last_sum,
        [jax.ShapeDtypeStruct(g.shape, jnp.bfloat16), line],
        [real_total, imag_total, first_term, second_term, before, dos, *seat_terms],
        [
            pltpu.VMEM(g.shape, jnp.bfloat16),
            pltpu.VMEM((1, m), jnp.float32),
            pltpu.SemaphoreType.DMA((pieces,)),
            pltpu.SemaphoreType.DMA,
        ],
        outside=(0, 1),
    )
    return sigma[None], cumulative


def solution(mesh):
    in_specs = (P("energy", "slab", None), P("slab", None), P(), P(), P())
    out_specs = (P("energy", "slab", None), P("energy", "slab"))
    return jax.shard_map(body, mesh=mesh, in_specs=in_specs, out_specs=out_specs, check_vma=False)
```
